256 devices in a mesh: stretch: 32 (over z_lo, x, core), seq: 8 (over z_hi, y).
Axes of the slice: x: 4, y: 4, z: 8 (z_hi: 2, z_lo: 4; z = z_hi * 4 + z_lo), core: 2. Of those that a mesh axis runs over, the one named last changes fastest.
Arguments:
- queries: bfloat16 [12288, 24, 128], P(('stretch', 'seq')), may hold values from -48 to 48
- keys_values: bfloat16 [12288, 8, 256], P(('stretch', 'seq')), may hold values from -12 to 12
- out_weight: bfloat16 [3072, 6144], P('seq'), may hold values from -0.109375 to 0.109375
- latents: bfloat16 [12288, 6144], P(('stretch', 'seq')), may hold values from -6 to 6
- gate_table: float32 [64, 6144], replicated, may hold values from 0.5 to 1.5
- noise_level: int32 [32], replicated, may hold values from 0 to 63
- stretch_mask: int32 [32, 32], replicated, may hold values from 0 to 1, as said below
Outputs:
- next_latents: bfloat16 [12288, 6144], P(('stretch', 'seq'))
The draws below stay inside these ranges and needn't reach their ends.
Inputs may be any that keep to these rules, and one draw needn't show every extreme that they name: stretch_mask[c, c] is 1 and stretch_mask[c, j] is 0 for j > c.
All inputs are finite; a program needn't handle non-finite values.
Results may differ from the reference program's by a relative error of at most 0.0095.
Values may be sent and summed in bfloat16 or wider, within the bound.
A program may use at most 64 MiB of HBM per device.

```python
import math
import jax
import jax.numpy as jnp
from jax import lax

D = 6144
HEADS = 24
KVH = 8
HD = 128
LEVELS = 64
CT = 384
STRETCHES = 32
TOKENS = 12288
N_SEQ = 8


def base_normal(key):
    return jax.random.truncated_normal(key, -3.7, 3.7, (TOKENS, KVH, HD), jnp.float32)


def draw_queries(key, part):
    key = jax.random.fold_in(key, 11)
    result = jax.random.truncated_normal(key, -3.7, 3.7, (TOKENS, HEADS, HD), jnp.float32)
    return result.astype(jnp.bfloat16)


def draw_keys_values(key, part):
    shared_normal = base_normal(key)
    key = jax.random.fold_in(key, 12)
    key_field = 3.0 * shared_normal
    value_field = jax.random.truncated_normal(key, -3.7, 3.7, (TOKENS, KVH, HD), jnp.float32)
    return jnp.concatenate([key_field, value_field], axis=-1).astype(jnp.bfloat16)


def draw_stretch_mask(key, part):
    key = jax.random.fold_in(key, 13)
    coins = jax.random.randint(key, (STRETCHES, STRETCHES), 0, 4)
    row_ids = jnp.arange(STRETCHES)[:, None]
    col_ids = jnp.arange(STRETCHES)[None, :]
    earlier = jnp.where(col_ids < row_ids, (coins > 0).astype(jnp.int32), 0)
    return jnp.where(row_ids == col_ids, 1, earlier).astype(jnp.int32)


def touch_ends(entries, rng, low, largest):
    place = [jax.random.randint(jax.random.fold_in(rng, axis), (), 0, length) for axis, length in enumerate(entries.shape)]
    widest = entries.shape.index(max(entries.shape))
    next_to = place[:widest] + [(place[widest] + 1) % entries.shape[widest]] + place[widest + 1:]
    return entries.at[tuple(place)].set(low).at[tuple(next_to)].set(largest)


def shard_levels(stream_key, shape, pieces, least, largest):
    def one(dim, blocks):
        steps = jax.random.uniform(jax.random.fold_in(jax.random.fold_in(stream_key, 6), dim), (blocks,), jnp.float32, least / len(pieces), largest / len(pieces))
        return jnp.repeat(jnp.exp(steps), shape[dim] // blocks).reshape((-1,) + (1,) * (len(shape) - dim - 1))

    gain = one(*pieces[0])
    for cut in pieces[1:]:
        gain = gain * one(*cut)
    return gain


def centred(stream_key, extent, scale, reach, pieces=(), kind=jnp.bfloat16):
    values = jax.random.normal(stream_key, extent, jnp.float32) * scale
    if len(pieces) > 0:
        values = shard_levels(stream_key, extent, pieces, -0.22, 0.18) * values
    return jnp.clip(values, min=-reach, max=reach).astype(kind)


def setup_inputs(seed: int = 0) -> dict:
    key_of = jax.random.split(jax.random.key(seed), 8)
    queries = draw_queries(jax.random.fold_in(key_of[7], 71), 0)
    keys_values = draw_keys_values(jax.random.fold_in(key_of[7], 71), 0)
    out_weight = centred(key_of[2], (HEADS * HD, D), (HEADS * HD) ** -0.5, 0.109375, ((0, 8),))
    latents = centred(key_of[3], (TOKENS, D), 1.0, 6.0, ((0, 256),))
    gate_table = jnp.clip(jax.random.uniform(key_of[4], (LEVELS, D), jnp.float32, 0.5, 1.5), 0.5, 1.5)
    noise_level = touch_ends(jax.random.randint(key_of[5], (STRETCHES,), 0, LEVELS), jax.random.fold_in(key_of[5], 1), 0, LEVELS - 1).astype(jnp.int32)
    stretch_mask = draw_stretch_mask(jax.random.fold_in(key_of[7], 71), 0)
    return dict(queries=queries, keys_values=keys_values, out_weight=out_weight, latents=latents, gate_table=gate_table, noise_level=noise_level, stretch_mask=stretch_mask)


def attend_block(att_carry, query_rows, kv_block):
    run_max, run_sum, accumulated = att_carry
    head_dim = query_rows.shape[-1]
    kv_heads = kv_block.shape[1]
    grouped = query_rows.reshape(query_rows.shape[0], kv_heads, -1, head_dim).astype(jnp.float32)
    key_part = kv_block[:, :, :head_dim].astype(jnp.float32)
    values = kv_block[:, :, head_dim:].astype(jnp.float32)
    scores = jnp.einsum('qkgd,pkd->kgqp', grouped, key_part) * (1.0 / math.sqrt(head_dim))
    new_max = jnp.maximum(run_max, lax.optimization_barrier(jnp.max(scores, axis=-1)))
    factor = jnp.exp(run_max - new_max)
    weights = jnp.exp(scores - new_max[..., None])
    run_sum = run_sum * factor + lax.optimization_barrier(jnp.sum(weights, axis=-1))
    rounded = lax.optimization_barrier(weights.astype(jnp.bfloat16)).astype(jnp.float32)
    update = jnp.einsum('kgqp,pkd->kgqd', rounded, values)
    accumulated = accumulated * factor[..., None] + update
    return (new_max, run_sum, accumulated)

def reference(queries, keys_values, out_weight, latents, gate_table, noise_level, stretch_mask):
    per_group = HEADS // KVH
    stretch_queries = queries.reshape(STRETCHES, CT, HEADS, HD)
    stretch_kv = keys_values.reshape(STRETCHES, CT, KVH, 2 * HD)

    def one_stretch(stretch_id):
        query_rows = stretch_queries[stretch_id]
        begin = (jnp.full((KVH, per_group, CT), -1e+30, jnp.float32), jnp.zeros((KVH, per_group, CT), jnp.float32), jnp.zeros((KVH, per_group, CT, HD), jnp.float32))

        def visit(source, current):
            return lax.cond(stretch_mask[stretch_id, source] == 1, lambda status: attend_block(status, query_rows, stretch_kv[source]), lambda status: status, current)
        run_max, run_sum, accumulated = lax.fori_loop(0, STRETCHES, visit, begin)
        result = accumulated / run_sum[..., None]
        return jnp.transpose(result, (2, 0, 1, 3)).reshape(CT, HEADS * HD).astype(jnp.bfloat16)
    attended = lax.map(one_stretch, jnp.arange(STRETCHES, dtype=jnp.int32)).reshape(TOKENS, HEADS * HD)
    block_width = HEADS * HD // N_SEQ
    branch = jnp.zeros((TOKENS, D), jnp.float32)
    for group_id in range(N_SEQ):
        partial_value = jnp.dot(attended[:, group_id * block_width:(group_id + 1) * block_width], out_weight[group_id * block_width:(group_id + 1) * block_width], preferred_element_type=jnp.float32)
        branch = branch + lax.optimization_barrier(partial_value.astype(jnp.bfloat16)).astype(jnp.float32)
    gate_rows = jnp.repeat(gate_table[noise_level], CT, axis=0)
    updated = (latents.astype(jnp.float32) + gate_rows * branch).astype(jnp.bfloat16)
    return jnp.roll(updated, CT, axis=0)
```

```python
import functools
import math

import jax
import jax.numpy as jnp
from jax import lax
from jax.experimental import pallas as pl
from jax.experimental.pallas import tpu as pltpu
from jax.sharding import PartitionSpec as P

MESH = pl.DeviceIdType.MESH
BIG = 1e30
MIB = 2**20

ROWS = 48
CT = 384
HD = 128
GROUP = 3
SEQ = 8
QROWS = CT * GROUP
D = 6144
EXP_SCALE = math.log2(math.e) / math.sqrt(HD)

NC = 4
CW = D // (2 * NC)


def position():
    c = lax.axis_index("stretch")
    s = lax.axis_index("seq")
    return c, s


def push(src, dst, send, recv, target):
    return pltpu.make_async_remote_copy(
        src_ref=src, dst_ref=dst, send_sem=send, recv_sem=recv, device_id=target, device_id_type=MESH
    )


def greet(targets):
    barrier = pltpu.get_barrier_semaphore()
    for target in targets:
        pl.semaphore_signal(barrier, inc=1, device_id=target, device_id_type=MESH)
    pl.semaphore_wait(barrier, len(targets))


def attention_kernel(
    q_ref, kv_ref, hide_ref, att_ref,
    kvr, qr, qt, slots, acc, run_max, run_sum,
    kv_send, kv_recv, q_send, q_recv, z_send, x_send, sib_send, slot_recv,
):
    c, s = position()
    z, x, k = c // 8, (c // 2) % 4, c % 2

    def dev(zz, xx, kk):
        return ((zz * 4 + xx) * 2 + kk, s)

    greet(
        [(c, (s + d) % SEQ) for d in range(1, SEQ)]
        + [dev((z + d) % 4, x, k) for d in (1, 2, 3)]
        + [dev(z, (x + d) % 4, k) for d in (1, 2, 3)]
        + [dev(z, x, 1 - k)]
    )

    def kv_copy(d):
        other = (s + d) % SEQ
        return push(kv_ref.at[other], kvr.at[s], kv_send.at[d], kv_recv.at[s], (c, other))

    def q_copy(d):
        other = (s + d) % SEQ
        return push(q_ref.at[other], qr.at[s], q_send.at[d], q_recv.at[s], (c, other))

    def landed(ref, recv, index):
        push(ref.at[index], ref.at[index], kv_send.at[0], recv.at[index], (c, (s + 1) % SEQ)).wait_recv()

    for d in (4, 3, 5, 2, 6, 1, 7):
        kv_copy(d).start()
    for d in (4, 3, 5, 2, 6, 1, 7):
        q_copy(d).start()
    kvr[s] = kv_ref[s]
    qr[s] = q_ref[s]
    run_max[...] = jnp.full_like(run_max, -BIG)
    run_sum[...] = jnp.zeros_like(run_sum)
    acc[...] = jnp.zeros_like(acc)
    for d in range(1, SEQ):
        landed(kvr, kv_recv, (s + d) % SEQ)
    block = kvr[...].reshape(CT, 2 * HD)
    slots[c, 0:CT, :] = block[:, :HD]
    value_t = jnp.transpose(block[:, HD:].astype(jnp.float32)).astype(jnp.bfloat16)
    for t in range(3):
        slots[c, CT + t * HD : CT + (t + 1) * HD, :] = value_t[:, t * HD : (t + 1) * HD]

    def slot_push(j, send, target):
        return push(slots.at[j], slots.at[j], send, slot_recv.at[j], target)

    def z_copy(d):
        return slot_push(c, z_send.at[d - 1], dev((z + d) % 4, x, k))

    def x_copy(t, d):
        return slot_push(dev(z - t, x, k)[0], x_send.at[t, d - 1], dev(z, (x + d) % 4, k))

    def pair_of(n):
        t, i = n // 4, n % 4
        step = i + i // 2 - 2 * (i // 3)
        return (z - t) * 4 + (x + step) % 4

    def sib_copy(n):
        return slot_push(2 * pair_of(n) + k, sib_send.at[n], dev(z, x, 1 - k))

    def wait_slot(j):
        slot_push(j, z_send.at[0], dev(z, x, 1 - k)).wait_recv()

    def spread(t):
        for d in (1, 3, 2):
            x_copy(t, d).start()
        sib_copy(4 * t).start()

    def forward(n):
        wait_slot(2 * pair_of(n) + k)
        sib_copy(n).start()

    sib_copy(0).start()
    for d in (1, 2, 3):
        @pl.when(z + d < 4)
        def _(d=d):
            z_copy(d).start()
    for d in (1, 3, 2):
        x_copy(0, d).start()

    for d in range(1, SEQ):
        landed(qr, q_recv, (s + d) % SEQ)
    qt[...] = jnp.transpose(qr[...].reshape(QROWS, HD).astype(jnp.float32)).astype(jnp.bfloat16)

    own_pair = z * 4 + x

    def attend(pair):
        ja = 2 * pair
        hide_a, hide_b = hide_ref[ja], hide_ref[ja + 1]

        def values(j):
            return jnp.concatenate(
                [slots[j, CT + t * HD : CT + (t + 1) * HD, :] for t in range(3)], axis=1
            )

        va, vb = values(ja), values(ja + 1)
        ka, kb = slots[ja, 0:CT, :], slots[ja + 1, 0:CT, :]
        for r in range(GROUP):
            cols = slice(r * CT, (r + 1) * CT)
            q_cols = qt[:, cols]
            sa = jnp.dot(ka, q_cols, preferred_element_type=jnp.float32)
            sb = jnp.dot(kb, q_cols, preferred_element_type=jnp.float32)
            top = jnp.maximum(
                jnp.max(sa, axis=0, keepdims=True) - hide_a, jnp.max(sb, axis=0, keepdims=True) - hide_b
            )
            old = run_max[:, cols]
            new = jnp.maximum(old, top)
            factor = jnp.exp2((old - new) * EXP_SCALE)
            pa = jnp.exp2((sa - (new + hide_a)) * EXP_SCALE)
            pb = jnp.exp2((sb - (new + hide_b)) * EXP_SCALE)
            run_max[:, cols] = new
            run_sum[:, cols] = (
                run_sum[:, cols] * factor
                + jnp.sum(pa, axis=0, keepdims=True)
                + jnp.sum(pb, axis=0, keepdims=True)
            )
            acc[:, cols] = (
                acc[:, cols] * factor
                + jnp.dot(va, pa.astype(jnp.bfloat16), preferred_element_type=jnp.float32)
                + jnp.dot(vb, pb.astype(jnp.bfloat16), preferred_element_type=jnp.float32)
            )

    def step(n, carry):
        t, i = n // 4, n % 4
        pair = pair_of(n)
        wait_slot(2 * pair + 1 - k)

        @pl.when(pair <= own_pair)
        def _():
            attend(pair)

        @pl.when((i == 0) & (t < z))
        def _():
            wait_slot(dev(z - t - 1, x, k)[0])
            spread(t + 1)

        @pl.when(n == 0)
        def _():
            forward(1)

        @pl.when((i < 2) | ((i == 3) & (t < z)))
        def _():
            forward(n + 2)

        return carry

    total = 4 * (z + 1)
    lax.fori_loop(0, total, step, 0)

    out = jnp.transpose(acc[...] * (1.0 / run_sum[...])).astype(jnp.bfloat16)
    att_ref[...] = out.reshape(SEQ, GROUP, ROWS, HD)

    for d in range(1, SEQ):
        kv_copy(d).wait_send()
        q_copy(d).wait_send()
    for d in (1, 2, 3):
        @pl.when(z + d < 4)
        def _(d=d):
            z_copy(d).wait_send()

    def drain_x(t, carry):
        for d in (1, 2, 3):
            x_copy(t, d).wait_send()
        return carry

    def drain_sib(n, carry):
        sib_copy(n).wait_send()
        return carry

    lax.fori_loop(0, z + 1, drain_x, 0)
    lax.fori_loop(0, total, drain_sib, 0)


def attention(q_t, kv_t, hide):
    flops = 4 * QROWS * HD * CT * 24
    return pl.pallas_call(
        attention_kernel,
        out_shape=jax.ShapeDtypeStruct((SEQ, GROUP, ROWS, HD), jnp.bfloat16),
        in_specs=[
            pl.BlockSpec(memory_space=pltpu.VMEM),
            pl.BlockSpec(memory_space=pltpu.VMEM),
            pl.BlockSpec(memory_space=pltpu.SMEM),
        ],
        out_specs=pl.BlockSpec(memory_space=pltpu.VMEM),
        scratch_shapes=[
            pltpu.VMEM((SEQ, ROWS, 2 * HD), jnp.bfloat16),
            pltpu.VMEM((SEQ, GROUP, ROWS, HD), jnp.bfloat16),
            pltpu.VMEM((HD, QROWS), jnp.bfloat16),
            pltpu.VMEM((32, 2 * CT, HD), jnp.bfloat16),
            pltpu.VMEM((HD, QROWS), jnp.float32),
            pltpu.VMEM((1, QROWS), jnp.float32),
            pltpu.VMEM((1, QROWS), jnp.float32),
            pltpu.SemaphoreType.DMA((SEQ,)),
            pltpu.SemaphoreType.DMA((SEQ,)),
            pltpu.SemaphoreType.DMA((SEQ,)),
            pltpu.SemaphoreType.DMA((SEQ,)),
            pltpu.SemaphoreType.DMA((3,)),
            pltpu.SemaphoreType.DMA((4, 3)),
            pltpu.SemaphoreType.DMA((16,)),
            pltpu.SemaphoreType.DMA((32,)),
        ],
        compiler_params=pltpu.CompilerParams(
            collective_id=0, has_side_effects=True, vmem_limit_bytes=32 * MIB
        ),
        cost_estimate=pl.CostEstimate(flops=flops, bytes_accessed=60 * MIB, transcendentals=QROWS * CT * 24),
        name="attention",
    )(q_t, kv_t, hide)


def project_kernel(
    att_ref, own_ref, other_ref, lat_ref, gate_ref, out_ref,
    att_in, weights, part, sends, recvs, done,
    w_sem, att_sem, ring_send, ring_recv, out_send, out_recv,
):
    c, s = position()
    zh, y = s // 4, s % 4
    partner = (c, (s + 4) % SEQ)
    up, down = (c, zh * 4 + (y + 1) % 4), (c, zh * 4 + (y + 3) % 4)
    after, before = ((c + 1) % 32, s), ((c + 31) % 32, s)

    def load(q):
        return [
            pltpu.make_async_copy(own_ref.at[:, pl.ds(q * CW, CW)], weights.at[0, q], w_sem.at[q, 0]),
            pltpu.make_async_copy(other_ref.at[2 * q], weights.at[1, q, :, 0:CT], w_sem.at[q, 1]),
            pltpu.make_async_copy(other_ref.at[2 * q + 1], weights.at[1, q, :, CT : 2 * CT], w_sem.at[q, 2]),
        ]

    for j in range(NC):
        for copy in load(j) + load(NC + j):
            copy.start()
    greet([partner, up, down, after, before])
    swap = push(
        att_ref.at[pl.ds(4 * (1 - zh), 4)], att_in, att_sem.at[0], att_sem.at[1], partner
    )
    swap.start()

    def ring(step, dirn, j):
        target = up if dirn == 0 else down
        return push(
            sends.at[step, dirn, j], recvs.at[step, dirn, j],
            ring_send.at[step, dirn, j], ring_recv.at[step, dirn, j], target,
        )

    def block_at(step, dirn):
        return (y + 3 - step) % 4 if dirn == 0 else (y + 1 + step) % 4

    def rows_of(att):
        heads = [att[:, h].reshape(4 * ROWS, HD) for h in range(GROUP)]
        return jnp.concatenate(heads, axis=1)

    own_rows = rows_of(att_ref[pl.ds(4 * zh, 4)])
    swap.wait()
    other_rows = rows_of(att_in[...])

    def first(j, carry):
        for dirn in range(2):
            q = dirn * NC + j
            for copy in load(q):
                copy.wait()
            product = jnp.dot(own_rows, weights[0, q], preferred_element_type=jnp.float32)
            product = product + jnp.dot(other_rows, weights[1, q], preferred_element_type=jnp.float32)
            part[q] = product.reshape(4, ROWS, CW)
            sends[0, dirn, j] = part[q, block_at(0, dirn)].astype(jnp.bfloat16)
            ring(0, dirn, j).start()
        return carry

    lax.fori_loop(0, NC, first, 0)

    for step in (1, 2):
        def middle(j, carry, step=step):
            for dirn in range(2):
                q = dirn * NC + j
                ring(step - 1, dirn, j).wait_recv()
                sends[step, dirn, j] = (
                    recvs[step - 1, dirn, j].astype(jnp.float32) + part[q, block_at(step, dirn)]
                ).astype(jnp.bfloat16)
                ring(step, dirn, j).start()
            return carry

        lax.fori_loop(0, NC, middle, 0)

    def final(q):
        cols = pl.ds(pl.multiple_of(q * CW, CW), CW)
        return push(done.at[:, cols], out_ref.at[:, cols], out_send.at[q], out_recv.at[q], after)

    def last(j, carry):
        for dirn in range(2):
            q = dirn * NC + j
            cols = pl.ds(pl.multiple_of(q * CW, CW), CW)
            ring(2, dirn, j).wait_recv()
            branch = recvs[2, dirn, j].astype(jnp.float32) + part[q, y]
            done[:, cols] = (
                lat_ref[:, cols].astype(jnp.float32) + gate_ref[:, cols] * branch
            ).astype(jnp.bfloat16)
            final(q).start()
        return carry

    lax.fori_loop(0, NC, last, 0)

    def drain(j, carry):
        for dirn in range(2):
            for step in range(3):
                ring(step, dirn, j).wait_send()
            final(dirn * NC + j).wait()
        return carry

    lax.fori_loop(0, NC, drain, 0)


def project(att, own, other, latents, gate_row):
    vmem = pl.BlockSpec(memory_space=pltpu.VMEM)
    anywhere = pl.BlockSpec(memory_space=pl.ANY)
    return pl.pallas_call(
        project_kernel,
        out_shape=jax.ShapeDtypeStruct((ROWS, D), jnp.bfloat16),
        in_specs=[vmem, anywhere, anywhere, vmem, vmem],
        out_specs=vmem,
        scratch_shapes=[
            pltpu.VMEM((4, GROUP, ROWS, HD), jnp.bfloat16),
            pltpu.VMEM((2, 2 * NC, CT, CW), jnp.bfloat16),
            pltpu.VMEM((2 * NC, 4, ROWS, CW), jnp.float32),
            pltpu.VMEM((3, 2, NC, ROWS, CW), jnp.bfloat16),
            pltpu.VMEM((3, 2, NC, ROWS, CW), jnp.bfloat16),
            pltpu.VMEM((ROWS, D), jnp.bfloat16),
            pltpu.SemaphoreType.DMA((2 * NC, 3)),
            pltpu.SemaphoreType.DMA((2,)),
            pltpu.SemaphoreType.DMA((3, 2, NC)),
            pltpu.SemaphoreType.DMA((3, 2, NC)),
            pltpu.SemaphoreType.DMA((2 * NC,)),
            pltpu.SemaphoreType.DMA((2 * NC,)),
        ],
        compiler_params=pltpu.CompilerParams(
            collective_id=1, has_side_effects=True, vmem_limit_bytes=40 * MIB
        ),
        cost_estimate=pl.CostEstimate(flops=4 * CT * CT * D, bytes_accessed=12 * MIB, transcendentals=0),
        name="project",
    )(att, own, other, latents, gate_row)


def partner_weights(out_weight, c):
    half, chip = c % 2, c // 2
    piece = lax.dynamic_slice(out_weight, (half * (CT // 2), chip * CT), (CT // 2, CT))
    piece = lax.ppermute(piece, "seq", [(i, (i + 4) % SEQ) for i in range(SEQ)])
    return lax.all_gather(piece, "stretch", axis=0, tiled=True).reshape(16, CT, CT)


def on_device(queries, keys_values, out_weight, latents, gate_table, noise_level, stretch_mask):
    c = lax.axis_index("stretch")
    other = partner_weights(out_weight, c)
    q_t = jnp.transpose(queries.reshape(ROWS, SEQ, GROUP, HD), (1, 2, 0, 3))
    kv_t = jnp.transpose(keys_values, (1, 0, 2))
    visible = lax.dynamic_index_in_dim(stretch_mask, c, 0, keepdims=False)
    hide = jnp.where(visible == 1, 0.0, BIG).astype(jnp.float32)
    att = attention(q_t, kv_t, hide)
    level = lax.dynamic_index_in_dim(noise_level, c, 0, keepdims=False)
    gate_row = lax.dynamic_slice(gate_table, (level, 0), (1, D))
    return project(att, out_weight, other, latents, gate_row)


def solution(mesh):
    rows = P(("stretch", "seq"), None)
    heads = P(("stretch", "seq"), None, None)
    return jax.shard_map(
        on_device,
        mesh=mesh,
        in_specs=(heads, heads, P("seq", None), rows, P(), P(), P()),
        out_specs=rows,
        check_vma=False,
    )
```

```python
import math

import jax
import jax.numpy as jnp
from jax import lax
from jax.experimental import pallas as pl
from jax.experimental.pallas import tpu as pltpu
from jax.sharding import PartitionSpec as P

MESH = pl.DeviceIdType.MESH
BIG = 1e30
MIB = 2**20
F32, BF16 = jnp.float32, jnp.bfloat16

ROWS = 48
CT = 384
HD = 128
GROUP = 3
SEQ = 8
QROWS = CT * GROUP
D = 6144
EXP_SCALE = math.log2(math.e) / math.sqrt(HD)

NC = 4
CW = D // (2 * NC)
CHUNKS = 16
DOWN = 10
HALF = CT // 2


def kernel(
    q_ref, kv_ref, mask_ref, level_ref, own_hbm, lat_hbm, gate_hbm, out_ref,
    kvr, qr, qt, slots, acc, run_max, run_sum, att, att_in, rows_in,
    own_w, other_w, part, sends, recvs, lat, gate, done,
    kv_send, kv_recv, q_send, q_recv, z_send, x_send, relay_send, sib_send, slot_recv, half_recv,
    load_sem, w_send, w_sib_send, w_recv, swap_sem, ring_send, ring_recv, out_send, out_recv,
):
    c = lax.axis_index("stretch")
    s = lax.axis_index("seq")
    z, x, k = c // 8, (c // 2) % 4, c % 2
    zh, y = s // 4, s % 4

    def dev(zz, xx, kk):
        return ((zz * 4 + xx) * 2 + kk, s)

    def z_next(step):
        pos = (zh * 4 + z + step + 8) % 8
        return (((pos % 4) * 4 + x) * 2 + k, (pos // 4) * 4 + y)

    sibling = dev(z, x, 1 - k)
    above, below = z_next(1), z_next(-1)
    x_right, x_left = dev(z, (x + 1) % 4, k), dev(z, (x + 3) % 4, k)
    partner = (c, (s + 4) % SEQ)
    y_up, y_down = (c, zh * 4 + (y + 1) % 4), (c, zh * 4 + (y + 3) % 4)
    after, before = ((c + 1) % 32, s), ((c + 31) % 32, s)

    def push(src, dst, send, recv, target):
        return pltpu.make_async_remote_copy(
            src_ref=src, dst_ref=dst, send_sem=send, recv_sem=recv, device_id=target, device_id_type=MESH
        )

    def load_own(b):
        return pltpu.make_async_copy(own_hbm.at[:, pl.ds(b * CT, CT)], own_w.at[b], load_sem.at[b])

    load_lat = pltpu.make_async_copy(lat_hbm, lat, load_sem.at[CHUNKS])
    load_gate = pltpu.make_async_copy(gate_hbm, gate, load_sem.at[CHUNKS + 1])

    barrier = pltpu.get_barrier_semaphore()
    greeted = [(c, (s + d) % SEQ) for d in range(1, SEQ)] + [
        above, below, x_right, x_left, sibling, after, before,
    ]
    for target in greeted:
        pl.semaphore_signal(barrier, inc=1, device_id=target, device_id_type=MESH)
    pl.semaphore_wait(barrier, len(greeted))

    def kv_copy(d):
        other = (s + d) % SEQ
        return push(kv_ref.at[other], kvr.at[s], kv_send.at[d], kv_recv.at[s], (c, other))

    def q_copy(d):
        other = (s + d) % SEQ
        return push(q_ref.at[other], qr.at[s], q_send.at[d], q_recv.at[s], (c, other))

    def landed(ref, recv, index):
        push(ref.at[index], ref.at[index], kv_send.at[0], recv.at[index], partner).wait_recv()

    for d in (4, 3, 5, 2, 6, 1, 7):
        kv_copy(d).start()
    for d in (4, 3, 5, 2, 6, 1, 7):
        q_copy(d).start()
    for b in range(CHUNKS):
        load_own(b).start()
    load_lat.start()
    load_gate.start()
    kvr[s] = kv_ref[s]
    qr[s] = q_ref[s]
    run_max[...] = jnp.full_like(run_max, -BIG)
    run_sum[...] = jnp.zeros_like(run_sum)
    acc[...] = jnp.zeros_like(acc)
    for d in range(1, SEQ):
        landed(kvr, kv_recv, (s + d) % SEQ)
    block = kvr[...].reshape(CT, 2 * HD)
    slots[c, 0:CT, :] = block[:, :HD]
    value_t = jnp.transpose(block[:, HD:].astype(F32)).astype(BF16)
    for t in range(3):
        slots[c, CT + t * HD : CT + (t + 1) * HD, :] = value_t[:, t * HD : (t + 1) * HD]

    def slot_push(j, send, target):
        return push(slots.at[j], slots.at[j], send, slot_recv.at[j], target)

    def column_slot(t):
        return ((z - t) * 4 + x) * 2 + k

    def z_copy(t):
        return slot_push(column_slot(t), z_send.at[t], above)

    def x_copy(t, right):
        return slot_push(column_slot(t), x_send.at[t, right], x_right if right else x_left)

    def pair_of(n):
        t, i = n // 4, n % 4
        step = i + i // 2 - 2 * (i // 3)
        return (z - t) * 4 + (x + step) % 4

    def sib_copy(n):
        return slot_push(2 * pair_of(n) + k, sib_send.at[n], sibling)

    def half_of(t, pair, right):
        part_of = slots.at[2 * pair + k, pl.ds(CT * right, CT)]
        return push(
            part_of, part_of, relay_send.at[t, right], half_recv.at[t, right], x_right if right else x_left
        )

    def relay(t, right):
        return half_of(t, (z - t) * 4 + (x + 1 + 2 * right) % 4, right)

    def wait_slot(j):
        slot_push(j, z_send.at[0], sibling).wait_recv()

    def spread(t):
        @pl.when(z < 3)
        def _():
            z_copy(t).start()

        x_copy(t, 0).start()
        x_copy(t, 1).start()
        sib_copy(4 * t).start()

    def from_beside(t, right):
        n = 4 * t + 1 + right
        wait_slot(2 * pair_of(n) + k)
        relay(t, right).start()
        sib_copy(n).start()

    def from_across(t):
        n = 4 * t + 3
        for right in range(2):
            half_of(t, pair_of(n), right).wait_recv()
        sib_copy(n).start()

    def w_slice(ref, half, u):
        return ref.at[half * 8 + u // 2, pl.ds((u % 2) * HALF, HALF)]

    def w_push(u, own, target):
        source = w_slice(own_w if own else other_w, k, u)
        return push(source, w_slice(other_w, k, u), w_send.at[u], w_recv.at[k, u], target)

    def w_sib(u):
        piece = w_slice(other_w, k, u)
        return push(piece, piece, w_sib_send.at[u], w_recv.at[k, u], sibling)

    def w_relay(u, edge, target):
        w_push(u, False, target).wait_recv()

        @pl.when(z != edge)
        def _():
            w_push(u, False, target).start()

        w_sib(u).start()

    spread(0)
    for d in range(1, SEQ):
        landed(qr, q_recv, (s + d) % SEQ)
    qt[...] = jnp.transpose(qr[...].reshape(QROWS, HD).astype(F32)).astype(BF16)
    for b in range(CHUNKS):
        load_own(b).wait()

    @pl.when(z == 0)
    def _():
        def origin(u, carry):
            w_push(u, True, below).start()
            return carry

        lax.fori_loop(0, DOWN, origin, 0)

    own_pair = z * 4 + x

    def attend(pair):
        ja = 2 * pair
        hide_a = jnp.where(mask_ref[c, ja] == 1, 0.0, BIG).astype(F32)
        hide_b = jnp.where(mask_ref[c, ja + 1] == 1, 0.0, BIG).astype(F32)
        ones = jnp.ones((16, CT), BF16)

        def values(j):
            cut = [slots[j, CT + t * HD : CT + (t + 1) * HD, :] for t in range(3)]
            return jnp.concatenate([jnp.concatenate(cut, axis=1), ones], axis=0)

        va, vb = values(ja), values(ja + 1)
        ka, kb = slots[ja, 0:CT, :], slots[ja + 1, 0:CT, :]

        def score(r):
            q_cols = qt[:, r * CT : (r + 1) * CT]
            return (
                jnp.dot(ka, q_cols, preferred_element_type=F32),
                jnp.dot(kb, q_cols, preferred_element_type=F32),
            )

        ready = score(0)
        for r in range(GROUP):
            ahead = score(r + 1) if r + 1 < GROUP else None
            sa, sb = ready
            cols = slice(r * CT, (r + 1) * CT)
            top = jnp.maximum(
                jnp.max(sa, axis=0, keepdims=True) - hide_a, jnp.max(sb, axis=0, keepdims=True) - hide_b
            )
            old = run_max[:, cols]
            new = jnp.maximum(old, top)
            factor = jnp.exp2((old - new) * EXP_SCALE)
            pa = jnp.exp2((sa - (new + hide_a)) * EXP_SCALE)
            pb = jnp.exp2((sb - (new + hide_b)) * EXP_SCALE)
            run_max[:, cols] = new
            update = jnp.dot(va, pa.astype(BF16), preferred_element_type=F32) + jnp.dot(
                vb, pb.astype(BF16), preferred_element_type=F32
            )
            run_sum[:, cols] = run_sum[:, cols] * factor + update[HD : HD + 1]
            acc[:, cols] = acc[:, cols] * factor + update[:HD]
            ready = ahead

    first_relay = 8 - 2 * z

    def step(n, carry):
        t, i = n // 4, n % 4
        pair = pair_of(n)
        wait_slot(2 * pair + 1 - k)

        @pl.when(pair <= own_pair)
        def _():
            attend(pair)

        @pl.when((i == 0) & (t < z))
        def _():
            wait_slot(column_slot(t + 1))
            spread(t + 1)

        @pl.when(n == 0)
        def _():
            from_beside(0, 0)
            from_beside(0, 1)

        @pl.when(i == 1)
        def _():
            from_across(t)

        @pl.when((i == 3) & (t < z))
        def _():
            from_beside(t + 1, 0)
            from_beside(t + 1, 1)

        @pl.when((z == 3) & (n < CHUNKS - DOWN))
        def _():
            w_push(DOWN + n, True, above).start()

        @pl.when((n >= first_relay) & (n % 2 == 0) & (n < first_relay + 2 * DOWN))
        def _():
            w_relay((n - first_relay) // 2, 0, below)

        return carry

    total = 4 * (z + 1)
    lax.fori_loop(0, total, step, 0)

    out = jnp.transpose(acc[...] * (1.0 / run_sum[...])).astype(BF16)
    att[...] = out.reshape(SEQ, GROUP, ROWS, HD)
    swap = push(att.at[pl.ds(4 * (1 - zh), 4)], att_in, swap_sem.at[0], swap_sem.at[1], partner)
    swap.start()

    def late(u, carry):
        @pl.when(u >= (6 * z - 3) // 2)
        def _():
            w_relay(u, 0, below)

        @pl.when(u < CHUNKS - DOWN)
        def _():
            w_relay(DOWN + u, 3, above)

        return carry

    lax.fori_loop(0, DOWN, late, 0)

    def gather_rows(source, first, place):
        for h in range(GROUP):
            rows_in[place, :, h * HD : (h + 1) * HD] = source[pl.ds(first, 4), h].reshape(4 * ROWS, HD)

    gather_rows(att, 4 * zh, 0)
    swap.wait()
    gather_rows(att_in, 0, 1)

    def ring(hop, dirn, j):
        return push(
            sends.at[hop, dirn, j], recvs.at[hop, dirn, j],
            ring_send.at[hop, dirn, j], ring_recv.at[hop, dirn, j], y_down if dirn else y_up,
        )

    def block_at(hop, dirn):
        return (y + 1 + hop) % 4 if dirn else (y + 3 - hop) % 4

    def first(j, carry):
        for b in range(4):
            w_from = w_slice(other_w, 1 - k, 4 * j + b)
            push(w_from, w_from, w_sib_send.at[0], w_recv.at[1 - k, 4 * j + b], sibling).wait_recv()
        for dirn in range(2):
            q = dirn * NC + j
            for b in range(2):
                product = jnp.dot(rows_in[0], own_w[2 * q + b], preferred_element_type=F32)
                product += jnp.dot(rows_in[1], other_w[2 * q + b], preferred_element_type=F32)
                part[q, :, :, b * CT : (b + 1) * CT] = product.reshape(4, ROWS, CT)
            sends[0, dirn, j] = part[q, block_at(0, dirn)].astype(BF16)
            ring(0, dirn, j).start()
        return carry

    lax.fori_loop(0, NC, first, 0)

    for hop in (1, 2):
        def middle(j, carry, hop=hop):
            for dirn in range(2):
                q = dirn * NC + j
                ring(hop - 1, dirn, j).wait_recv()
                sends[hop, dirn, j] = (
                    recvs[hop - 1, dirn, j].astype(F32) + part[q, block_at(hop, dirn)]
                ).astype(BF16)
                ring(hop, dirn, j).start()
            return carry

        lax.fori_loop(0, NC, middle, 0)

    load_lat.wait()
    load_gate.wait()
    level = level_ref[c]

    def final(q):
        cols = pl.ds(pl.multiple_of(q * CW, CW), CW)
        return push(done.at[:, cols], out_ref.at[:, cols], out_send.at[q], out_recv.at[q], after)

    def last(j, carry):
        for dirn in range(2):
            q = dirn * NC + j
            cols = pl.ds(pl.multiple_of(q * CW, CW), CW)
            ring(2, dirn, j).wait_recv()
            branch = recvs[2, dirn, j].astype(F32) + part[q, y]
            gate_row = gate[pl.ds(level, 1), cols]
            done[:, cols] = (lat[:, cols].astype(F32) + gate_row * branch).astype(BF16)
            final(q).start()
        return carry

    lax.fori_loop(0, NC, last, 0)

    for d in range(1, SEQ):
        kv_copy(d).wait_send()
        q_copy(d).wait_send()

    def drain_plane(t, carry):
        @pl.when(z < 3)
        def _():
            z_copy(t).wait_send()

        for right in range(2):
            x_copy(t, right).wait_send()
            relay(t, right).wait_send()
        return carry

    def drain_sib(n, carry):
        sib_copy(n).wait_send()
        return carry

    def drain_w(u, carry):
        w_push(u, False, below).wait_send()
        w_sib(u).wait_send()
        return carry

    def drain_ring(j, carry):
        for dirn in range(2):
            for hop in range(3):
                ring(hop, dirn, j).wait_send()
            final(dirn * NC + j).wait()
        return carry

    lax.fori_loop(0, z + 1, drain_plane, 0)
    lax.fori_loop(0, total, drain_sib, 0)
    lax.fori_loop(0, CHUNKS, drain_w, 0)
    lax.fori_loop(0, NC, drain_ring, 0)


def fused(q_t, kv_t, mask, level, own, latents, gate_table):
    vmem = pl.BlockSpec(memory_space=pltpu.VMEM)
    smem = pl.BlockSpec(memory_space=pltpu.SMEM)
    anywhere = pl.BlockSpec(memory_space=pl.ANY)
    dma = pltpu.SemaphoreType.DMA
    return pl.pallas_call(
        kernel,
        out_shape=jax.ShapeDtypeStruct((ROWS, D), BF16),
        in_specs=[vmem, vmem, smem, smem, anywhere, anywhere, anywhere],
        out_specs=vmem,
        scratch_shapes=[
            pltpu.VMEM((SEQ, ROWS, 2 * HD), BF16),
            pltpu.VMEM((SEQ, GROUP, ROWS, HD), BF16),
            pltpu.VMEM((HD, QROWS), BF16),
            pltpu.VMEM((32, 2 * CT, HD), BF16),
            pltpu.VMEM((HD, QROWS), F32),
            pltpu.VMEM((1, QROWS), F32),
            pltpu.VMEM((1, QROWS), F32),
            pltpu.VMEM((SEQ, GROUP, ROWS, HD), BF16),
            pltpu.VMEM((4, GROUP, ROWS, HD), BF16),
            pltpu.VMEM((2, 4 * ROWS, CT), BF16),
            pltpu.VMEM((CHUNKS, CT, CT), BF16),
            pltpu.VMEM((CHUNKS, CT, CT), BF16),
            pltpu.VMEM((2 * NC, 4, ROWS, CW), F32),
            pltpu.VMEM((3, 2, NC, ROWS, CW), BF16),
            pltpu.VMEM((3, 2, NC, ROWS, CW), BF16),
            pltpu.VMEM((ROWS, D), BF16),
            pltpu.VMEM((64, D), F32),
            pltpu.VMEM((ROWS, D), BF16),
            dma((SEQ,)), dma((SEQ,)), dma((SEQ,)), dma((SEQ,)),
            dma((4,)), dma((4, 2)), dma((4, 2)), dma((16,)), dma((32,)), dma((4, 2)),
            dma((CHUNKS + 2,)), dma((CHUNKS,)), dma((CHUNKS,)), dma((2, CHUNKS)), dma((2,)),
            dma((3, 2, NC)), dma((3, 2, NC)), dma((2 * NC,)), dma((2 * NC,)),
        ],
        compiler_params=pltpu.CompilerParams(
            collective_id=0, has_side_effects=True, vmem_limit_bytes=48 * MIB
        ),
        cost_estimate=pl.CostEstimate(
            flops=4 * QROWS * HD * CT * 24, bytes_accessed=20 * MIB, transcendentals=QROWS * CT * 24
        ),
        name="stretch_attention",
    )(q_t, kv_t, mask, level, own, latents, gate_table)


def on_device(queries, keys_values, out_weight, latents, gate_table, noise_level, stretch_mask):
    q_t = jnp.transpose(queries.reshape(ROWS, SEQ, GROUP, HD), (1, 2, 0, 3))
    kv_t = jnp.transpose(keys_values, (1, 0, 2))
    return fused(q_t, kv_t, stretch_mask, noise_level, out_weight, latents, gate_table)


def solution(mesh):
    rows = P(("stretch", "seq"), None)
    heads = P(("stretch", "seq"), None, None)
    return jax.shard_map(
        on_device,
        mesh=mesh,
        in_specs=(heads, heads, P("seq", None), rows, P(), P(), P()),
        out_specs=rows,
        check_vma=False,
    )
```

```python
import math

import jax
import jax.numpy as jnp
from jax import lax
from jax.experimental import pallas as pl
from jax.experimental.pallas import tpu as pltpu
from jax.sharding import PartitionSpec as P

MESH = pl.DeviceIdType.MESH
BIG = 1e30
MIB = 2**20
F32, BF16 = jnp.float32, jnp.bfloat16

ROWS = 48
CT = 384
HD = 128
GROUP = 3
SEQ = 8
QROWS = CT * GROUP
D = 6144
EXP_SCALE = math.log2(math.e) / math.sqrt(HD)

NC = 8
BLOCKS = 16


def kernel(
    q_ref, kv_ref, mask_ref, level_ref, own_hbm, lat_hbm, gate_hbm, out_ref,
    kvr, qr, qt, slots, acc, run_max, run_sum, att, att_in, rows_in,
    own_w, other_w, part, sends, recvs, lat, gate, done,
    kv_send, kv_recv, q_send, q_recv, z_send, x_send, relay_send, sib_send, slot_recv, half_recv,
    load_sem, w_edge_send, w_send, w_sib_send, w_recv, swap_sem, ring_send, ring_recv, out_send, out_recv,
):
    c = lax.axis_index("stretch")
    s = lax.axis_index("seq")
    z, x, k = c // 8, (c // 2) % 4, c % 2
    zh, y = s // 4, s % 4

    def dev(zz, xx, kk):
        return ((zz * 4 + xx) * 2 + kk, s)

    def z_next(step):
        pos = (zh * 4 + z + step + 8) % 8
        return (((pos % 4) * 4 + x) * 2 + k, (pos // 4) * 4 + y)

    sibling = dev(z, x, 1 - k)
    above = z_next(1)
    outward = 2 * (z // 3) - 1
    x_right, x_left, x_across = (dev(z, (x + d) % 4, k) for d in (1, 3, 2))
    partner = (c, (s + 4) % SEQ)
    y_up, y_down = (c, zh * 4 + (y + 1) % 4), (c, zh * 4 + (y + 3) % 4)
    after, before = ((c + 1) % 32, s), ((c + 31) % 32, s)

    def push(src, dst, send, recv, target):
        return pltpu.make_async_remote_copy(
            src_ref=src, dst_ref=dst, send_sem=send, recv_sem=recv, device_id=target, device_id_type=MESH
        )

    def load_own(b):
        return pltpu.make_async_copy(own_hbm.at[:, pl.ds(b * CT, CT)], own_w.at[b], load_sem.at[b])

    load_lat = pltpu.make_async_copy(lat_hbm, lat, load_sem.at[BLOCKS])
    load_gate = pltpu.make_async_copy(gate_hbm, gate, load_sem.at[BLOCKS + 1])

    barrier = pltpu.get_barrier_semaphore()
    greeted = [(c, (s + d) % SEQ) for d in range(1, SEQ)] + [
        z_next(1), z_next(-1), z_next(2), z_next(-2), x_right, x_left, x_across, sibling, after, before,
    ]
    for target in greeted:
        pl.semaphore_signal(barrier, inc=1, device_id=target, device_id_type=MESH)
    pl.semaphore_wait(barrier, len(greeted))

    def kv_copy(d):
        other = (s + d) % SEQ
        return push(kv_ref.at[other], kvr.at[s], kv_send.at[d], kv_recv.at[s], (c, other))

    def q_copy(d):
        other = (s + d) % SEQ
        return push(q_ref.at[other], qr.at[s], q_send.at[d], q_recv.at[s], (c, other))

    def landed(ref, recv, index):
        push(ref.at[index], ref.at[index], kv_send.at[0], recv.at[index], partner).wait_recv()

    for d in (4, 3, 5, 2, 6, 1, 7):
        kv_copy(d).start()
    for d in (4, 3, 5, 2, 6, 1, 7):
        q_copy(d).start()
    for b in range(BLOCKS):
        load_own(b).start()
    load_lat.start()
    load_gate.start()
    kvr[s] = kv_ref[s]
    qr[s] = q_ref[s]
    run_max[...] = jnp.full_like(run_max, -BIG)
    run_sum[...] = jnp.zeros_like(run_sum)
    acc[...] = jnp.zeros_like(acc)
    for d in range(1, SEQ):
        landed(kvr, kv_recv, (s + d) % SEQ)
    block = kvr[...].reshape(CT, 2 * HD)
    slots[c, 0:CT, :] = block[:, :HD]
    value_t = jnp.transpose(block[:, HD:].astype(F32)).astype(BF16)
    for t in range(3):
        slots[c, CT + t * HD : CT + (t + 1) * HD, :] = value_t[:, t * HD : (t + 1) * HD]

    def slot_push(j, send, target):
        return push(slots.at[j], slots.at[j], send, slot_recv.at[j], target)

    def column_slot(t):
        return ((z - t) * 4 + x) * 2 + k

    def z_copy(t):
        return slot_push(column_slot(t), z_send.at[t], above)

    def x_copy(t, right):
        return slot_push(column_slot(t), x_send.at[t, right], x_right if right else x_left)

    def pair_of(n):
        t, i = n // 4, n % 4
        step = i + i // 2 - 2 * (i // 3)
        return (z - t) * 4 + (x + step) % 4

    def sib_copy(n):
        return slot_push(2 * pair_of(n) + k, sib_send.at[n], sibling)

    def half_of(t, pair, right):
        part_of = slots.at[2 * pair + k, pl.ds(CT * right, CT)]
        return push(
            part_of, part_of, relay_send.at[t, right], half_recv.at[t, right], x_right if right else x_left
        )

    def relay(t, right):
        return half_of(t, (z - t) * 4 + (x + 1 + 2 * right) % 4, right)

    def wait_slot(j):
        slot_push(j, z_send.at[0], sibling).wait_recv()

    def spread(t):
        @pl.when(z < 3)
        def _():
            z_copy(t).start()

        x_copy(t, 0).start()
        x_copy(t, 1).start()
        sib_copy(4 * t).start()

    def from_beside(t, right):
        n = 4 * t + 1 + right
        wait_slot(2 * pair_of(n) + k)
        relay(t, right).start()
        sib_copy(n).start()

    def from_across(t):
        n = 4 * t + 3
        for right in range(2):
            half_of(t, pair_of(n), right).wait_recv()
        sib_copy(n).start()

    def block_of(place):
        group = place // 4
        step = group + group // 2 - 2 * (group // 3)
        return 4 * ((x + step) % 4) + place % 4

    def w_push(source, b, send, target):
        return push(source.at[b], other_w.at[b], send, w_recv.at[b], target)

    def w_edge(half, hop):
        return w_push(own_w, 4 * x + 2 * k + half, w_edge_send.at[half, hop - 1], z_next(hop * outward))

    def w_side(half, way):
        target = (x_right, x_left, x_across, sibling)[way]
        return w_push(other_w, 4 * x + 2 * k + half, w_send.at[half, way], target)

    def w_sib(group, half):
        return w_push(other_w, block_of(4 * group) + 2 * k + half, w_sib_send.at[group, half], sibling)

    def w_wait(b):
        w_push(other_w, b, w_send.at[0, 0], sibling).wait_recv()

    def w_spread(half):
        w_wait(4 * x + 2 * k + half)
        for way in range(4):
            w_side(half, way).start()

    def w_hand_over(group):
        for half in range(2):
            w_wait(block_of(4 * group) + 2 * k + half)
            w_sib(group, half).start()

    spread(0)
    for d in range(1, SEQ):
        landed(qr, q_recv, (s + d) % SEQ)
    qt[...] = jnp.transpose(qr[...].reshape(QROWS, HD).astype(F32)).astype(BF16)
    for b in range(BLOCKS):
        load_own(b).wait()

    @pl.when(z % 3 == 0)
    def _():
        for half in range(2):
            for hop in (1, 2):
                w_edge(half, hop).start()

    own_pair = z * 4 + x

    def attend(pair):
        ja = 2 * pair
        hide_a = jnp.where(mask_ref[c, ja] == 1, 0.0, BIG).astype(F32)
        hide_b = jnp.where(mask_ref[c, ja + 1] == 1, 0.0, BIG).astype(F32)
        ones = jnp.ones((16, CT), BF16)

        def values(j):
            cut = [slots[j, CT + t * HD : CT + (t + 1) * HD, :] for t in range(3)]
            return jnp.concatenate([jnp.concatenate(cut, axis=1), ones], axis=0)

        va, vb = values(ja), values(ja + 1)
        ka, kb = slots[ja, 0:CT, :], slots[ja + 1, 0:CT, :]

        def score(r):
            q_cols = qt[:, r * CT : (r + 1) * CT]
            return (
                jnp.dot(ka, q_cols, preferred_element_type=F32),
                jnp.dot(kb, q_cols, preferred_element_type=F32),
            )

        ready = score(0)
        for r in range(GROUP):
            ahead = score(r + 1) if r + 1 < GROUP else None
            sa, sb = ready
            cols = slice(r * CT, (r + 1) * CT)
            top = jnp.maximum(
                jnp.max(sa, axis=0, keepdims=True) - hide_a, jnp.max(sb, axis=0, keepdims=True) - hide_b
            )
            old = run_max[:, cols]
            new = jnp.maximum(old, top)
            factor = jnp.exp2((old - new) * EXP_SCALE)
            pa = jnp.exp2((sa - (new + hide_a)) * EXP_SCALE)
            pb = jnp.exp2((sb - (new + hide_b)) * EXP_SCALE)
            run_max[:, cols] = new
            update = jnp.dot(va, pa.astype(BF16), preferred_element_type=F32) + jnp.dot(
                vb, pb.astype(BF16), preferred_element_type=F32
            )
            run_sum[:, cols] = run_sum[:, cols] * factor + update[HD : HD + 1]
            acc[:, cols] = acc[:, cols] * factor + update[:HD]
            ready = ahead

    def pass_on(t):
        wait_slot(column_slot(t))
        spread(t)

    def step(n, carry):
        t, i = n // 4, n % 4
        pair = pair_of(n)
        wait_slot(2 * pair + 1 - k)

        @pl.when(pair <= own_pair)
        def _():
            attend(pair)

        @pl.when(n == 0)
        def _():
            from_beside(0, 0)
            from_beside(0, 1)

        for ahead, at in ((1, 0), (2, 2), (3, 5)):
            @pl.when((n == at) & (z >= ahead))
            def _(ahead=ahead):
                pass_on(ahead)

        @pl.when((n == 2) | ((i == 1) & (t > 0)))
        def _():
            from_across(t)

        @pl.when((i == 3) & (t < z))
        def _():
            from_beside(t + 1, 0)
            from_beside(t + 1, 1)

        @pl.when(n == 4 * z + 1 - 4 * (z // 3))
        def _():
            w_spread(0)

        @pl.when(n == 4 * z + 3 - 2 * (z // 3))
        def _():
            w_spread(1)

        return carry

    total = 4 * (z + 1)
    lax.fori_loop(0, total, step, 0)

    out = jnp.transpose(acc[...] * (1.0 / run_sum[...])).astype(BF16)
    att[...] = out.reshape(SEQ, GROUP, ROWS, HD)
    swap = push(att.at[pl.ds(4 * (1 - zh), 4)], att_in, swap_sem.at[0], swap_sem.at[1], partner)
    swap.start()

    def gather_rows(source, first, place):
        for h in range(GROUP):
            rows_in[place, :, h * HD : (h + 1) * HD] = source[pl.ds(first, 4), h].reshape(4 * ROWS, HD)

    gather_rows(att, 4 * zh, 0)
    swap.wait()
    gather_rows(att_in, 0, 1)

    def ring(hop, dirn, j):
        return push(
            sends.at[hop, dirn, j], recvs.at[hop, dirn, j],
            ring_send.at[hop, dirn, j], ring_recv.at[hop, dirn, j], y_down if dirn else y_up,
        )

    def block_at(hop, dirn):
        return (y + 1 + hop) % 4 if dirn else (y + 3 - hop) % 4

    def first(j, carry):
        @pl.when(j % 2 != k)
        def _():
            for dirn in range(2):
                w_wait(block_of(2 * j + dirn))

        for dirn in range(2):
            q = block_of(2 * j + dirn)
            product = jnp.dot(rows_in[0], own_w[q], preferred_element_type=F32)
            product += jnp.dot(rows_in[1], other_w[q], preferred_element_type=F32)
            part[dirn, j] = product.reshape(4, ROWS, CT)
            sends[0, dirn, j] = part[dirn, j, block_at(0, dirn)].astype(BF16)
            ring(0, dirn, j).start()

        @pl.when((j % 2 == 0) & (j < 6))
        def _():
            w_hand_over(j // 2 + 1)

        return carry

    lax.fori_loop(0, NC, first, 0)

    for hop in (1, 2):
        def middle(j, carry, hop=hop):
            for dirn in range(2):
                ring(hop - 1, dirn, j).wait_recv()
                sends[hop, dirn, j] = (
                    recvs[hop - 1, dirn, j].astype(F32) + part[dirn, j, block_at(hop, dirn)]
                ).astype(BF16)
                ring(hop, dirn, j).start()
            return carry

        lax.fori_loop(0, NC, middle, 0)

    load_lat.wait()
    load_gate.wait()
    level = level_ref[c]

    def columns(place):
        return pl.ds(pl.multiple_of(block_of(place) * CT, CT), CT)

    def final(place):
        cols = columns(place)
        return push(done.at[:, cols], out_ref.at[:, cols], out_send.at[place], out_recv.at[place], after)

    def last(j, carry):
        for dirn in range(2):
            cols = columns(2 * j + dirn)
            ring(2, dirn, j).wait_recv()
            branch = recvs[2, dirn, j].astype(F32) + part[dirn, j, y]
            gate_row = gate[pl.ds(level, 1), cols]
            done[:, cols] = (lat[:, cols].astype(F32) + gate_row * branch).astype(BF16)
            final(2 * j + dirn).start()
        return carry

    lax.fori_loop(0, NC, last, 0)

    for d in range(1, SEQ):
        kv_copy(d).wait_send()
        q_copy(d).wait_send()

    def drain_plane(t, carry):
        @pl.when(z < 3)
        def _():
            z_copy(t).wait_send()

        for right in range(2):
            x_copy(t, right).wait_send()
            relay(t, right).wait_send()
        return carry

    def drain_sib(n, carry):
        sib_copy(n).wait_send()
        return carry

    @pl.when(z % 3 == 0)
    def _():
        for half in range(2):
            for hop in (1, 2):
                w_edge(half, hop).wait_send()

    for half in range(2):
        for way in range(4):
            w_side(half, way).wait_send()
        for group in (1, 2, 3):
            w_sib(group, half).wait_send()

    def drain_ring(j, carry):
        for dirn in range(2):
            for hop in range(3):
                ring(hop, dirn, j).wait_send()
            final(2 * j + dirn).wait()
        return carry

    lax.fori_loop(0, z + 1, drain_plane, 0)
    lax.fori_loop(0, total, drain_sib, 0)
    lax.fori_loop(0, NC, drain_ring, 0)


def fused(q_t, kv_t, mask, level, own, latents, gate_table):
    vmem = pl.BlockSpec(memory_space=pltpu.VMEM)
    smem = pl.BlockSpec(memory_space=pltpu.SMEM)
    anywhere = pl.BlockSpec(memory_space=pl.ANY)
    dma = pltpu.SemaphoreType.DMA
    return pl.pallas_call(
        kernel,
        out_shape=jax.ShapeDtypeStruct((ROWS, D), BF16),
        in_specs=[vmem, vmem, smem, smem, anywhere, anywhere, anywhere],
        out_specs=vmem,
        scratch_shapes=[
            pltpu.VMEM((SEQ, ROWS, 2 * HD), BF16),
            pltpu.VMEM((SEQ, GROUP, ROWS, HD), BF16),
            pltpu.VMEM((HD, QROWS), BF16),
            pltpu.VMEM((32, 2 * CT, HD), BF16),
            pltpu.VMEM((HD, QROWS), F32),
            pltpu.VMEM((1, QROWS), F32),
            pltpu.VMEM((1, QROWS), F32),
            pltpu.VMEM((SEQ, GROUP, ROWS, HD), BF16),
            pltpu.VMEM((4, GROUP, ROWS, HD), BF16),
            pltpu.VMEM((2, 4 * ROWS, CT), BF16),
            pltpu.VMEM((BLOCKS, CT, CT), BF16),
            pltpu.VMEM((BLOCKS, CT, CT), BF16),
            pltpu.VMEM((2, NC, 4, ROWS, CT), F32),
            pltpu.VMEM((3, 2, NC, ROWS, CT), BF16),
            pltpu.VMEM((3, 2, NC, ROWS, CT), BF16),
            pltpu.VMEM((ROWS, D), BF16),
            pltpu.VMEM((64, D), F32),
            pltpu.VMEM((ROWS, D), BF16),
            dma((SEQ,)), dma((SEQ,)), dma((SEQ,)), dma((SEQ,)),
            dma((4,)), dma((4, 2)), dma((4, 2)), dma((16,)), dma((32,)), dma((4, 2)),
            dma((BLOCKS + 2,)), dma((2, 2)), dma((2, 4)), dma((4, 2)), dma((BLOCKS,)), dma((2,)),
            dma((3, 2, NC)), dma((3, 2, NC)), dma((BLOCKS,)), dma((BLOCKS,)),
        ],
        compiler_params=pltpu.CompilerParams(
            collective_id=0, has_side_effects=True, vmem_limit_bytes=48 * MIB
        ),
        cost_estimate=pl.CostEstimate(
            flops=4 * QROWS * HD * CT * 24, bytes_accessed=20 * MIB, transcendentals=QROWS * CT * 24
        ),
        name="stretch_attention",
    )(q_t, kv_t, mask, level, own, latents, gate_table)


def on_device(queries, keys_values, out_weight, latents, gate_table, noise_level, stretch_mask):
    q_t = jnp.transpose(queries.reshape(ROWS, SEQ, GROUP, HD), (1, 2, 0, 3))
    kv_t = jnp.transpose(keys_values, (1, 0, 2))
    return fused(q_t, kv_t, stretch_mask, noise_level, out_weight, latents, gate_table)


def solution(mesh):
    rows = P(("stretch", "seq"), None)
    heads = P(("stretch", "seq"), None, None)
    return jax.shard_map(
        on_device,
        mesh=mesh,
        in_specs=(heads, heads, P("seq", None), rows, P(), P(), P()),
        out_specs=rows,
        check_vma=False,
    )
```

```python
import math

import jax
import jax.numpy as jnp
from jax import lax
from jax.experimental import pallas as pl
from jax.experimental.pallas import tpu as pltpu
from jax.sharding import PartitionSpec as P

MESH = pl.DeviceIdType.MESH
BIG = 1e30
MIB = 2**20
F32, BF16 = jnp.float32, jnp.bfloat16

ROWS = 48
CT = 384
HD = 128
GROUP = 3
SEQ = 8
QROWS = CT * GROUP
D = 6144
EXP_SCALE = math.log2(math.e) / math.sqrt(HD)

NC = 8
BLOCKS = 16


def kernel(
    q_raw, kv_raw, mask_hbm, level_hbm, own_hbm, lat_hbm, gate_hbm, out_ref,
    q_ref, kv_ref, mask_ref, level_ref, kvr, qr, qt, slots, acc, run_max, run_sum, att, att_in, rows_in,
    own_w, other_w, part, sends, recvs, lat, gate, done,
    kv_send, kv_recv, q_send, q_recv, z_send, x_send, relay_send, sib_send, slot_recv, half_recv,
    load_sem, w_edge_send, w_send, w_sib_send, w_recv, swap_sem, ring_send, ring_recv, out_send, out_recv,
):
    c = lax.axis_index("stretch")
    s = lax.axis_index("seq")
    z, x, k = c // 8, (c // 2) % 4, c % 2
    zh, y = s // 4, s % 4

    def dev(zz, xx, kk):
        return ((zz * 4 + xx) * 2 + kk, s)

    def z_next(step):
        pos = (zh * 4 + z + step + 8) % 8
        return (((pos % 4) * 4 + x) * 2 + k, (pos // 4) * 4 + y)

    sibling = dev(z, x, 1 - k)
    above = z_next(1)
    outward = 2 * (z // 3) - 1
    x_right, x_left = dev(z, (x + 1) % 4, k), dev(z, (x + 3) % 4, k)
    partner = (c, (s + 4) % SEQ)
    y_up, y_down = (c, zh * 4 + (y + 1) % 4), (c, zh * 4 + (y + 3) % 4)
    after, before = ((c + 1) % 32, s), ((c + 31) % 32, s)

    def push(src, dst, send, recv, target):
        return pltpu.make_async_remote_copy(
            src_ref=src, dst_ref=dst, send_sem=send, recv_sem=recv, device_id=target, device_id_type=MESH
        )

    def load_own(b):
        return pltpu.make_async_copy(own_hbm.at[:, pl.ds(b * CT, CT)], own_w.at[b], load_sem.at[b])

    load_lat = pltpu.make_async_copy(lat_hbm, lat, load_sem.at[BLOCKS])
    load_gate = pltpu.make_async_copy(gate_hbm, gate, load_sem.at[BLOCKS + 1])
    load_mask = pltpu.make_async_copy(mask_hbm, mask_ref, load_sem.at[BLOCKS + 2])
    load_level = pltpu.make_async_copy(level_hbm, level_ref, load_sem.at[BLOCKS + 3])

    barrier = pltpu.get_barrier_semaphore()
    greeted = [(c, (s + d) % SEQ) for d in range(1, SEQ)] + [
        z_next(1), z_next(-1), x_right, x_left, sibling, after, before,
    ]
    for target in greeted:
        pl.semaphore_signal(barrier, inc=1, device_id=target, device_id_type=MESH)
    load_mask.start()
    load_level.start()
    for b in range(BLOCKS):
        load_own(b).start()
    load_lat.start()
    load_gate.start()
    kv_ref[...] = jnp.transpose(kv_raw[...], (1, 0, 2))
    q_ref[...] = jnp.transpose(q_raw[...], (1, 0, 2)).reshape(SEQ, GROUP, ROWS, HD)
    run_max[...] = jnp.full_like(run_max, -BIG)
    run_sum[...] = jnp.zeros_like(run_sum)
    acc[...] = jnp.zeros_like(acc)
    kvr[s] = kv_ref[s]
    qr[s] = q_ref[s]
    pl.semaphore_wait(barrier, len(greeted))

    def kv_copy(d):
        other = (s + d) % SEQ
        return push(kv_ref.at[other], kvr.at[s], kv_send.at[d], kv_recv.at[s], (c, other))

    def q_copy(d):
        other = (s + d) % SEQ
        return push(q_ref.at[other], qr.at[s], q_send.at[d], q_recv.at[s], (c, other))

    def landed(ref, recv, index):
        push(ref.at[index], ref.at[index], kv_send.at[0], recv.at[index], partner).wait_recv()

    for d in (4, 3, 5, 2, 6, 1, 7):
        kv_copy(d).start()
    for d in (4, 3, 5, 2, 6, 1, 7):
        q_copy(d).start()
    for d in range(1, SEQ):
        landed(kvr, kv_recv, (s + d) % SEQ)
    block = kvr[...].reshape(CT, 2 * HD)
    slots[c, 0:CT, :] = block[:, :HD]
    value_t = jnp.transpose(block[:, HD:].astype(F32)).astype(BF16)
    for t in range(3):
        slots[c, CT + t * HD : CT + (t + 1) * HD, :] = value_t[:, t * HD : (t + 1) * HD]

    def slot_push(j, send, target):
        return push(slots.at[j], slots.at[j], send, slot_recv.at[j], target)

    def column_slot(t):
        return ((z - t) * 4 + x) * 2 + k

    def z_copy(t):
        return slot_push(column_slot(t), z_send.at[t], above)

    def x_copy(t, right):
        return slot_push(column_slot(t), x_send.at[t, right], x_right if right else x_left)

    def pair_of(n):
        t, i = n // 4, n % 4
        step = i + i // 2 - 2 * (i // 3)
        return (z - t) * 4 + (x + step) % 4

    def sib_copy(n):
        return slot_push(2 * pair_of(n) + k, sib_send.at[n], sibling)

    def half_of(t, pair, right):
        part_of = slots.at[2 * pair + k, pl.ds(CT * right, CT)]
        return push(
            part_of, part_of, relay_send.at[t, right], half_recv.at[t, right], x_right if right else x_left
        )

    def relay(t, right):
        return half_of(t, (z - t) * 4 + (x + 1 + 2 * right) % 4, right)

    def wait_slot(j):
        slot_push(j, z_send.at[0], sibling).wait_recv()

    def spread(t):
        @pl.when(z < 3)
        def _():
            z_copy(t).start()

        x_copy(t, 0).start()
        x_copy(t, 1).start()
        sib_copy(4 * t).start()

    def from_beside(t, right):
        n = 4 * t + 1 + right
        wait_slot(2 * pair_of(n) + k)
        relay(t, right).start()
        sib_copy(n).start()

    def from_across(t):
        n = 4 * t + 3
        for right in range(2):
            half_of(t, pair_of(n), right).wait_recv()
        sib_copy(n).start()

    def block_of(place):
        return 8 * ((x + place // 8) % 2) + place % 8

    def w_push(source, b, send, target):
        return push(source.at[b], other_w.at[b], send, w_recv.at[b], target)

    def core_block(b):
        return block_of(8 * (b // 4) + 4 * ((b // 2) % 2) + 2 * k + b % 2)

    def w_edge(b):
        return w_push(own_w, core_block(b), w_edge_send.at[b], z_next(outward))

    def w_inward(b):
        return w_push(other_w, core_block(b), w_send.at[b, 0], z_next(-outward))

    def w_beside(b):
        return w_push(other_w, core_block(b), w_send.at[b, 1], dev(z, (x + 1 + 2 * (b // 2)) % 4, k))

    def w_sib(b):
        return w_push(other_w, core_block(b), w_sib_send.at[b], sibling)

    def w_wait(b):
        w_push(other_w, b, w_sib_send.at[0], sibling).wait_recv()

    def w_spread(b):
        w_wait(core_block(b))

        @pl.when(z % 3 == 0)
        def _():
            w_inward(b).start()

        w_beside(b).start()
        w_sib(b).start()

    def w_hand_over(b):
        w_wait(core_block(b))
        w_sib(b).start()

    def pass_on(t):
        wait_slot(column_slot(t))
        spread(t)

    spread(0)
    from_beside(0, 0)
    from_beside(0, 1)

    @pl.when(z >= 1)
    def _():
        pass_on(1)

    for d in range(1, SEQ):
        landed(qr, q_recv, (s + d) % SEQ)
    qt[...] = jnp.transpose(qr[...].reshape(QROWS, HD).astype(F32)).astype(BF16)
    for b in range(BLOCKS):
        load_own(b).wait()

    @pl.when(z % 3 == 0)
    def _():
        for b in range(4):
            w_edge(b).start()

    load_mask.wait()
    load_level.wait()

    own_pair = z * 4 + x

    def attend(pair):
        ja = 2 * pair
        hide_a = jnp.where(mask_ref[c, ja] == 1, 0.0, BIG).astype(F32)
        hide_b = jnp.where(mask_ref[c, ja + 1] == 1, 0.0, BIG).astype(F32)
        ones = jnp.ones((16, CT), BF16)

        def values(j):
            cut = [slots[j, CT + t * HD : CT + (t + 1) * HD, :] for t in range(3)]
            return jnp.concatenate([jnp.concatenate(cut, axis=1), ones], axis=0)

        va, vb = values(ja), values(ja + 1)
        ka, kb = slots[ja, 0:CT, :], slots[ja + 1, 0:CT, :]

        def score(r):
            q_cols = qt[:, r * CT : (r + 1) * CT]
            return (
                jnp.dot(ka, q_cols, preferred_element_type=F32),
                jnp.dot(kb, q_cols, preferred_element_type=F32),
            )

        ready = score(0)
        for r in range(GROUP):
            ahead = score(r + 1) if r + 1 < GROUP else None
            sa, sb = ready
            cols = slice(r * CT, (r + 1) * CT)
            top = jnp.maximum(
                jnp.max(sa, axis=0, keepdims=True) - hide_a, jnp.max(sb, axis=0, keepdims=True) - hide_b
            )
            old = run_max[:, cols]
            new = jnp.maximum(old, top)
            factor = jnp.exp2((old - new) * EXP_SCALE)
            pa = jnp.exp2((sa - (new + hide_a)) * EXP_SCALE)
            pb = jnp.exp2((sb - (new + hide_b)) * EXP_SCALE)
            run_max[:, cols] = new
            update = jnp.dot(va, pa.astype(BF16), preferred_element_type=F32) + jnp.dot(
                vb, pb.astype(BF16), preferred_element_type=F32
            )
            run_sum[:, cols] = run_sum[:, cols] * factor + update[HD : HD + 1]
            acc[:, cols] = acc[:, cols] * factor + update[:HD]
            ready = ahead

    def step(n, carry):
        t, i = n // 4, n % 4
        pair = pair_of(n)
        wait_slot(2 * pair + 1 - k)

        @pl.when(pair <= own_pair)
        def _():
            attend(pair)

        for ahead, at in ((2, 1), (3, 4)):
            @pl.when((n == at) & (z >= ahead))
            def _(ahead=ahead):
                pass_on(ahead)

        @pl.when(i == 1)
        def _():
            from_across(t)

        @pl.when((i == 3) & (t < z))
        def _():
            from_beside(t + 1, 0)
            from_beside(t + 1, 1)

        @pl.when((z == 3) & (n >= 4) & (n % 3 == 1))
        def _():
            w_spread((n - 4) // 3)

        @pl.when((z < 3) & (n >= 4 * z) & (n % 2 == 1))
        def _():
            w_spread((n - 4 * z) // 2)

        return carry

    total = 4 * (z + 1)
    lax.fori_loop(0, total, step, 0)

    out = jnp.transpose(acc[...] * (1.0 / run_sum[...])).astype(BF16)
    att[...] = out.reshape(SEQ, GROUP, ROWS, HD)
    swap = push(att.at[pl.ds(4 * (1 - zh), 4)], att_in, swap_sem.at[0], swap_sem.at[1], partner)
    swap.start()

    @pl.when(z < 3)
    def _():
        w_spread(2)
        w_spread(3)

    def gather_rows(source, first, place):
        for h in range(GROUP):
            rows_in[place, :, h * HD : (h + 1) * HD] = source[pl.ds(first, 4), h].reshape(4 * ROWS, HD)

    gather_rows(att, 4 * zh, 0)
    swap.wait()
    gather_rows(att_in, 0, 1)

    def ring(hop, dirn, j):
        return push(
            sends.at[hop, dirn, j], recvs.at[hop, dirn, j],
            ring_send.at[hop, dirn, j], ring_recv.at[hop, dirn, j], y_down if dirn else y_up,
        )

    def block_at(hop, dirn):
        return (y + 1 + hop) % 4 if dirn else (y + 3 - hop) % 4

    def first(j, carry):
        @pl.when(j % 2 != k)
        def _():
            for dirn in range(2):
                w_wait(block_of(2 * j + dirn))

        for dirn in range(2):
            q = block_of(2 * j + dirn)
            product = jnp.dot(rows_in[0], own_w[q], preferred_element_type=F32)
            product += jnp.dot(rows_in[1], other_w[q], preferred_element_type=F32)
            part[dirn, j] = product.reshape(4, ROWS, CT)
            sends[0, dirn, j] = part[dirn, j, block_at(0, dirn)].astype(BF16)
            ring(0, dirn, j).start()

        @pl.when((j == 1) | (j == 3))
        def _():
            w_hand_over(3 + j)
            w_hand_over(4 + j)

        return carry

    lax.fori_loop(0, NC, first, 0)

    for hop in (1, 2):
        def middle(j, carry, hop=hop):
            for dirn in range(2):
                ring(hop - 1, dirn, j).wait_recv()
                sends[hop, dirn, j] = (
                    recvs[hop - 1, dirn, j].astype(F32) + part[dirn, j, block_at(hop, dirn)]
                ).astype(BF16)
                ring(hop, dirn, j).start()
            return carry

        lax.fori_loop(0, NC, middle, 0)

    load_lat.wait()
    load_gate.wait()
    level = level_ref[c]

    def columns(place):
        return pl.ds(pl.multiple_of(block_of(place) * CT, CT), CT)

    def final(place):
        cols = columns(place)
        return push(done.at[:, cols], out_ref.at[:, cols], out_send.at[place], out_recv.at[place], after)

    def last(j, carry):
        for dirn in range(2):
            cols = columns(2 * j + dirn)
            ring(2, dirn, j).wait_recv()
            branch = recvs[2, dirn, j].astype(F32) + part[dirn, j, y]
            gate_row = gate[pl.ds(level, 1), cols]
            done[:, cols] = (lat[:, cols].astype(F32) + gate_row * branch).astype(BF16)
            final(2 * j + dirn).start()
        return carry

    lax.fori_loop(0, NC, last, 0)

    for d in range(1, SEQ):
        kv_copy(d).wait_send()
        q_copy(d).wait_send()

    def drain_plane(t, carry):
        @pl.when(z < 3)
        def _():
            z_copy(t).wait_send()

        for right in range(2):
            x_copy(t, right).wait_send()
            relay(t, right).wait_send()
        return carry

    def drain_sib(n, carry):
        sib_copy(n).wait_send()
        return carry

    for b in range(4):
        @pl.when(z % 3 == 0)
        def _(b=b):
            w_edge(b).wait_send()
            w_inward(b).wait_send()

        w_beside(b).wait_send()
    for b in range(8):
        w_sib(b).wait_send()

    def drain_ring(j, carry):
        for dirn in range(2):
            for hop in range(3):
                ring(hop, dirn, j).wait_send()
            final(2 * j + dirn).wait()
        return carry

    lax.fori_loop(0, z + 1, drain_plane, 0)
    lax.fori_loop(0, total, drain_sib, 0)
    lax.fori_loop(0, NC, drain_ring, 0)


def fused(queries, keys_values, mask, level, own, latents, gate_table):
    vmem = pl.BlockSpec(memory_space=pltpu.VMEM)
    anywhere = pl.BlockSpec(memory_space=pl.ANY)
    dma = pltpu.SemaphoreType.DMA
    return pl.pallas_call(
        kernel,
        out_shape=jax.ShapeDtypeStruct((ROWS, D), BF16),
        in_specs=[vmem, vmem] + [anywhere] * 5,
        out_specs=vmem,
        scratch_shapes=[
            pltpu.VMEM((SEQ, GROUP, ROWS, HD), BF16),
            pltpu.VMEM((SEQ, ROWS, 2 * HD), BF16),
            pltpu.SMEM((32, 32), jnp.int32),
            pltpu.SMEM((32,), jnp.int32),
            pltpu.VMEM((SEQ, ROWS, 2 * HD), BF16),
            pltpu.VMEM((SEQ, GROUP, ROWS, HD), BF16),
            pltpu.VMEM((HD, QROWS), BF16),
            pltpu.VMEM((32, 2 * CT, HD), BF16),
            pltpu.VMEM((HD, QROWS), F32),
            pltpu.VMEM((1, QROWS), F32),
            pltpu.VMEM((1, QROWS), F32),
            pltpu.VMEM((SEQ, GROUP, ROWS, HD), BF16),
            pltpu.VMEM((4, GROUP, ROWS, HD), BF16),
            pltpu.VMEM((2, 4 * ROWS, CT), BF16),
            pltpu.VMEM((BLOCKS, CT, CT), BF16),
            pltpu.VMEM((BLOCKS, CT, CT), BF16),
            pltpu.VMEM((2, NC, 4, ROWS, CT), F32),
            pltpu.VMEM((3, 2, NC, ROWS, CT), BF16),
            pltpu.VMEM((3, 2, NC, ROWS, CT), BF16),
            pltpu.VMEM((ROWS, D), BF16),
            pltpu.VMEM((64, D), F32),
            pltpu.VMEM((ROWS, D), BF16),
            dma((SEQ,)), dma((SEQ,)), dma((SEQ,)), dma((SEQ,)),
            dma((4,)), dma((4, 2)), dma((4, 2)), dma((16,)), dma((32,)), dma((4, 2)),
            dma((BLOCKS + 4,)), dma((4,)), dma((4, 2)), dma((8,)), dma((BLOCKS,)), dma((2,)),
            dma((3, 2, NC)), dma((3, 2, NC)), dma((BLOCKS,)), dma((BLOCKS,)),
        ],
        compiler_params=pltpu.CompilerParams(
            collective_id=0, has_side_effects=True, vmem_limit_bytes=60 * MIB
        ),
        cost_estimate=pl.CostEstimate(
            flops=4 * QROWS * HD * CT * 24, bytes_accessed=20 * MIB, transcendentals=QROWS * CT * 24
        ),
        name="stretch_attention",
    )(queries, keys_values, mask, level, own, latents, gate_table)


def on_device(queries, keys_values, out_weight, latents, gate_table, noise_level, stretch_mask):
    return fused(queries, keys_values, stretch_mask, noise_level, out_weight, latents, gate_table)


def solution(mesh):
    rows = P(("stretch", "seq"), None)
    heads = P(("stretch", "seq"), None, None)
    return jax.shard_map(
        on_device,
        mesh=mesh,
        in_specs=(heads, heads, P("seq", None), rows, P(), P(), P()),
        out_specs=rows,
        check_vma=False,
    )
```

```python
import math

import jax
import jax.numpy as jnp
from jax import lax
from jax.experimental import pallas as pl
from jax.experimental.pallas import tpu as pltpu
from jax.sharding import PartitionSpec as P

MESH = pl.DeviceIdType.MESH
BIG = 1e30
MIB = 2**20
F32, BF16 = jnp.float32, jnp.bfloat16

ROWS = 48
CT = 384
HD = 128
GROUP = 3
SEQ = 8
QROWS = CT * GROUP
D = 6144
EXP_SCALE = math.log2(math.e) / math.sqrt(HD)

NC = 8
LAG = 2
BLOCKS = 16


def kernel(
    q_raw, kv_raw, mask_hbm, level_hbm, own_hbm, lat_hbm, gate_hbm, out_ref,
    q_ref, kv_ref, mask_ref, level_ref, q_far, att_far, mate_att, blend, lse, lse_partner, lse_mate, kvr, qr, qt, slots, acc, run_max, run_sum, att, att_in, rows_in,
    own_w, other_w, part, sends, recvs, lat, gate, done,
    mate_send, mate_recv, kv_send, kv_recv, q_send, q_recv, z_send, down_send, x_send, relay_send, sib_send, slot_recv, half_recv,
    load_sem, w_edge_send, w_send, w_sib_send, w_recv, swap_sem, ring_send, ring_recv, out_send, out_recv,
):
    c = lax.axis_index("stretch")
    s = lax.axis_index("seq")
    z, x, k = c // 8, (c // 2) % 4, c % 2
    zh, y = s // 4, s % 4
    bottom = 1 - (z + 3) // 4
    planes = 2 + z // 2 - z // 3

    def dev(zz, xx, kk):
        return ((zz * 4 + xx) * 2 + kk, s)

    def z_next(step):
        pos = (zh * 4 + z + step + 8) % 8
        return (((pos % 4) * 4 + x) * 2 + k, (pos // 4) * 4 + y)

    sibling = dev(z, x, 1 - k)
    above = z_next(1)
    outward = 2 * (z // 3) - 1
    mate = dev(3 - z, x, k)
    x_right, x_left, x_across = (dev(z, (x + d) % 4, k) for d in (1, 3, 2))
    partner = (c, (s + 4) % SEQ)
    y_up, y_down = (c, zh * 4 + (y + 1) % 4), (c, zh * 4 + (y + 3) % 4)
    after, before = ((c + 1) % 32, s), ((c + 31) % 32, s)

    def push(src, dst, send, recv, target):
        return pltpu.make_async_remote_copy(
            src_ref=src, dst_ref=dst, send_sem=send, recv_sem=recv, device_id=target, device_id_type=MESH
        )

    def load_own(b):
        return pltpu.make_async_copy(own_hbm.at[:, pl.ds(b * CT, CT)], own_w.at[b], load_sem.at[b])

    load_lat = pltpu.make_async_copy(lat_hbm, lat, load_sem.at[BLOCKS])
    load_gate = pltpu.make_async_copy(gate_hbm, gate, load_sem.at[BLOCKS + 1])
    load_mask = pltpu.make_async_copy(mask_hbm, mask_ref, load_sem.at[BLOCKS + 2])
    load_level = pltpu.make_async_copy(level_hbm, level_ref, load_sem.at[BLOCKS + 3])

    barrier = pltpu.get_barrier_semaphore()
    greeted = [(c, (s + d) % SEQ) for d in range(1, SEQ)] + [
        z_next(1), z_next(-1), x_right, x_left, x_across, sibling, mate,
        after, before,
    ]
    for target in greeted:
        pl.semaphore_signal(barrier, inc=1, device_id=target, device_id_type=MESH)
    load_mask.start()
    load_level.start()
    for b in range(BLOCKS):
        load_own(b).start()
    load_lat.start()
    load_gate.start()
    kv_ref[...] = jnp.transpose(kv_raw[...], (1, 0, 2))
    q_ref[...] = jnp.transpose(q_raw[...], (1, 0, 2)).reshape(SEQ, GROUP, ROWS, HD)
    run_max[...] = jnp.full_like(run_max, -BIG)
    run_sum[...] = jnp.zeros_like(run_sum)
    acc[...] = jnp.zeros_like(acc)
    kvr[s] = kv_ref[s]
    qr[s] = q_ref[s]
    pl.semaphore_wait(barrier, len(greeted))

    def kv_copy(d):
        other = (s + d) % SEQ
        return push(kv_ref.at[other], kvr.at[s], kv_send.at[d], kv_recv.at[s], (c, other))

    def q_copy(d):
        other = (s + d) % SEQ
        return push(q_ref.at[other], qr.at[s], q_send.at[d], q_recv.at[s], (c, other))

    def landed(ref, recv, index):
        push(ref.at[index], ref.at[index], kv_send.at[0], recv.at[index], partner).wait_recv()

    for d in (4, 3, 5, 2, 6, 1, 7):
        kv_copy(d).start()
    for d in range(1, SEQ):
        landed(kvr, kv_recv, (s + d) % SEQ)
    block = kvr[...].reshape(CT, 2 * HD)
    slots[c, 0:CT, :] = block[:, :HD]
    value_t = jnp.transpose(block[:, HD:].astype(F32)).astype(BF16)
    for t in range(3):
        slots[c, CT + t * HD : CT + (t + 1) * HD, :] = value_t[:, t * HD : (t + 1) * HD]

    def slot_push(j, send, target):
        return push(slots.at[j], slots.at[j], send, slot_recv.at[j], target)

    def plane_of(t):
        return z - t + 2 * t * bottom

    def column_slot(t):
        return (plane_of(t) * 4 + x) * 2 + k

    def z_copy(t):
        return slot_push(column_slot(t), z_send.at[t], above)

    def x_copy(t, right):
        return slot_push(column_slot(t), x_send.at[t, right], x_right if right else x_left)

    def pair_of(n):
        t, i = n // 4, n % 4
        step = i + i // 2 - 2 * (i // 3)
        return plane_of(t) * 4 + (x + step) % 4

    def sib_copy(n):
        return slot_push(2 * pair_of(n) + k, sib_send.at[n], sibling)

    def half_of(t, pair, right):
        part_of = slots.at[2 * pair + k, pl.ds(CT * right, CT)]
        return push(
            part_of, part_of, relay_send.at[t, right], half_recv.at[t, right], x_right if right else x_left
        )

    def relay(t, right):
        return half_of(t, plane_of(t) * 4 + (x + 1 + 2 * right) % 4, right)

    def wait_slot(j):
        slot_push(j, z_send.at[0], sibling).wait_recv()

    def down_copy():
        return slot_push(column_slot(0), down_send.at[0], z_next(-1))

    def spread(t):
        @pl.when((z == 1) | ((z % 2 == 0) & (t == 0)))
        def _():
            z_copy(t).start()

        @pl.when((z == 1) & (t == 0))
        def _():
            down_copy().start()

        x_copy(t, 0).start()
        x_copy(t, 1).start()
        sib_copy(4 * t).start()

    def from_beside(t, right):
        n = 4 * t + 1 + right
        wait_slot(2 * pair_of(n) + k)
        relay(t, right).start()
        sib_copy(n).start()

    def from_across(t):
        n = 4 * t + 3
        for right in range(2):
            half_of(t, pair_of(n), right).wait_recv()
        sib_copy(n).start()

    def block_of(place):
        group = place // 4
        step = group + group // 2 - 2 * (group // 3)
        return 4 * ((x + step) % 4) + place % 4

    def w_push(source, b, send, target):
        return push(source.at[b], other_w.at[b], send, w_recv.at[b], target)

    def core_block(b):
        return block_of(4 * (b // 2) + 2 * k + b % 2)

    def w_edge(b):
        return w_push(own_w, core_block(b), w_edge_send.at[b], z_next(outward))

    def w_inward(b):
        return w_push(other_w, core_block(b), w_send.at[b, 0], z_next(-outward))

    def w_beside(b, way):
        target = (x_right, x_left, x_across)[way]
        return w_push(other_w, core_block(b), w_send.at[b, 1 + way], target)

    def w_sib(b):
        return w_push(other_w, core_block(b), w_sib_send.at[b], sibling)

    def w_wait(b):
        w_push(other_w, b, w_sib_send.at[0], sibling).wait_recv()

    def w_spread(b):
        w_wait(core_block(b))

        @pl.when(z % 3 == 0)
        def _():
            w_inward(b).start()

        for way in range(3):
            w_beside(b, way).start()
        w_sib(b).start()

    def w_hand_over(b):
        w_wait(core_block(b))
        w_sib(b).start()

    def pass_on(t):
        wait_slot(column_slot(t))
        spread(t)

    spread(0)
    for d in (4, 3, 5, 2, 6, 1, 7):
        q_copy(d).start()
    from_beside(0, 0)
    from_beside(0, 1)

    pass_on(1)

    for d in range(1, SEQ):
        landed(qr, q_recv, (s + d) % SEQ)
    q_mate = push(qr, q_far, mate_send.at[0], mate_recv.at[0], mate)

    @pl.when(z == 3)
    def _():
        q_mate.start()

    def take_queries(source):
        qt[...] = jnp.transpose(source[...].reshape(QROWS, HD).astype(F32)).astype(BF16)

    take_queries(qr)
    for b in range(BLOCKS):
        load_own(b).wait()

    @pl.when(z % 3 == 0)
    def _():
        for b in range(2):
            w_edge(b).start()

    load_mask.wait()
    load_level.wait()

    own_pair = z * 4 + x
    swap = push(att.at[pl.ds(4 * (1 - zh), 4)], att_in, swap_sem.at[0], swap_sem.at[1], partner)
    lse_swap = push(lse, lse_partner, mate_send.at[1], mate_recv.at[1], partner)

    def mate_part(near, target):
        half = zh if near else 1 - zh
        at = 0 if near else 1
        return (
            push(att_far.at[pl.ds(4 * half, 4)], mate_att.at[at], mate_send.at[2 + at], mate_recv.at[2 + at], target),
            push(lse, lse_mate.at[at], mate_send.at[4 + at], mate_recv.at[4 + at], target),
        )

    def finish(target):
        total_weight = jnp.maximum(run_sum[...], 1e-30)
        out = jnp.transpose(acc[...] * (1.0 / total_weight)).astype(BF16)
        target[...] = out.reshape(SEQ, GROUP, ROWS, HD)
        lse[...] = jnp.broadcast_to(run_max[...] * EXP_SCALE + jnp.log2(total_weight), lse.shape)

    def attend(pair, row):
        ja = 2 * pair
        hide_a = jnp.where(mask_ref[row, ja] == 1, 0.0, 2 * BIG).astype(F32)
        hide_b = jnp.where(mask_ref[row, ja + 1] == 1, 0.0, 2 * BIG).astype(F32)
        ones = jnp.ones((16, CT), BF16)

        def values(j):
            cut = [slots[j, CT + t * HD : CT + (t + 1) * HD, :] for t in range(3)]
            return jnp.concatenate([jnp.concatenate(cut, axis=1), ones], axis=0)

        va, vb = values(ja), values(ja + 1)
        ka, kb = slots[ja, 0:CT, :], slots[ja + 1, 0:CT, :]

        def score(r):
            q_cols = qt[:, r * CT : (r + 1) * CT]
            return (
                jnp.dot(ka, q_cols, preferred_element_type=F32),
                jnp.dot(kb, q_cols, preferred_element_type=F32),
            )

        ready = score(0)
        for r in range(GROUP):
            ahead = score(r + 1) if r + 1 < GROUP else None
            sa, sb = ready
            cols = slice(r * CT, (r + 1) * CT)
            top = jnp.maximum(
                jnp.max(sa, axis=0, keepdims=True) - hide_a, jnp.max(sb, axis=0, keepdims=True) - hide_b
            )
            old = run_max[:, cols]
            new = jnp.maximum(old, top)
            factor = jnp.exp2((old - new) * EXP_SCALE)
            pa = jnp.exp2((sa - (new + hide_a)) * EXP_SCALE)
            pb = jnp.exp2((sb - (new + hide_b)) * EXP_SCALE)
            run_max[:, cols] = new
            update = jnp.dot(va, pa.astype(BF16), preferred_element_type=F32) + jnp.dot(
                vb, pb.astype(BF16), preferred_element_type=F32
            )
            run_sum[:, cols] = run_sum[:, cols] * factor + update[HD : HD + 1]
            acc[:, cols] = acc[:, cols] * factor + update[:HD]
            ready = ahead

    w_first = jnp.where(z == 2, 8, 3)
    w_count = jnp.where(z == 1, 0, 2)

    def step(n, carry):
        t, i = (n // 4) // (1 + bottom), n % 4
        fresh = (bottom == 0) | (n // 4 != 1)
        for_mate = (bottom == 1) & (n >= 4)
        pair = pair_of(4 * t + i)

        @pl.when((bottom == 1) & (n == 4))
        def _():
            finish(att)
            swap.start()
            q_mate.wait_recv()
            take_queries(q_far)
            run_max[...] = jnp.full_like(run_max, -BIG)
            run_sum[...] = jnp.zeros_like(run_sum)
            acc[...] = jnp.zeros_like(acc)

        @pl.when(fresh)
        def _():
            wait_slot(2 * pair + 1 - k)

        @pl.when((pair <= own_pair) | for_mate)
        def _():
            attend(pair, c + 24 * bottom * ((n + 8) // 12))

        @pl.when((n == 1) & (z == 2))
        def _():
            pass_on(2)

        @pl.when((i == 1) & fresh)
        def _():
            from_across(t)

        @pl.when((i == 3) & (n // 4 + 1 < planes))
        def _():
            from_beside(n // 4 + 1, 0)
            from_beside(n // 4 + 1, 1)

        turn = n - w_first

        @pl.when((turn >= 0) & (turn % 3 == 0) & (turn < 3 * w_count))
        def _():
            w_spread(turn // 3)

        return carry

    lax.fori_loop(0, 4 * (planes + bottom), step, 0)

    @pl.when(z == 0)
    def _():
        finish(att_far)
        for copy in mate_part(True, mate) + mate_part(False, z_next(-1)):
            copy.start()

    @pl.when(z != 0)
    def _():
        finish(att)
        swap.start()

    @pl.when(z == 3)
    def _():
        lse_swap.start()

    @pl.when(w_count == 0)
    def _():
        w_spread(0)
        w_spread(1)

    def gather_rows(source, first, place):
        for h in range(GROUP):
            rows_in[place, :, h * HD : (h + 1) * HD] = source[pl.ds(first, 4), h].reshape(4 * ROWS, HD)

    def blended(near, lse_home, lse_far, home, far):
        top = jnp.maximum(lse_home, lse_far)
        home_weight, far_weight = jnp.exp2(lse_home - top), jnp.exp2(lse_far - top)
        share = jnp.broadcast_to(home_weight / (home_weight + far_weight), (HD, QROWS))
        blend[...] = jnp.transpose(share).reshape(SEQ, GROUP, ROWS, HD)
        part_of = blend[pl.ds(4 * zh, 4)]
        mixed = part_of * home.astype(F32) + (1.0 - part_of) * far.astype(F32)
        return mixed.astype(BF16)

    swap.wait()

    @pl.when(z == 3)
    def _():
        lse_swap.wait()
        for copy in mate_part(True, mate) + mate_part(False, mate):
            copy.wait_recv()
        att[pl.ds(4 * zh, 4)] = blended(True, lse[0:1], lse_mate[0, 0:1], att[pl.ds(4 * zh, 4)], mate_att[0])
        att_in[...] = blended(False, lse_partner[0:1], lse_mate[1, 0:1], att_in[...], mate_att[1])

    gather_rows(att, 4 * zh, 0)
    gather_rows(att_in, 0, 1)

    def ring(hop, dirn, j):
        return push(
            sends.at[hop, dirn, j], recvs.at[hop, dirn, j],
            ring_send.at[hop, dirn, j], ring_recv.at[hop, dirn, j], y_down if dirn else y_up,
        )

    def block_at(hop, dirn):
        return (y + 1 + hop) % 4 if dirn else (y + 3 - hop) % 4

    def columns(place):
        return pl.ds(pl.multiple_of(block_of(place) * CT, CT), CT)

    def final(place):
        cols = columns(place)
        return push(done.at[:, cols], out_ref.at[:, cols], out_send.at[place], out_recv.at[place], after)

    load_lat.wait()
    load_gate.wait()
    level = level_ref[c]

    def first(j):
        @pl.when(j % 2 != k)
        def _():
            for dirn in range(2):
                w_wait(block_of(2 * j + dirn))

        for dirn in range(2):
            q = block_of(2 * j + dirn)
            product = jnp.dot(rows_in[0], own_w[q], preferred_element_type=F32)
            product += jnp.dot(rows_in[1], other_w[q], preferred_element_type=F32)
            part[dirn, j] = product.reshape(4, ROWS, CT)
            sends[0, dirn, j] = part[dirn, j, block_at(0, dirn)].astype(BF16)
            ring(0, dirn, j).start()

    def middle(hop, j):
        for dirn in range(2):
            ring(hop - 1, dirn, j).wait_recv()
            sends[hop, dirn, j] = (
                recvs[hop - 1, dirn, j].astype(F32) + part[dirn, j, block_at(hop, dirn)]
            ).astype(BF16)
            ring(hop, dirn, j).start()

    def last(j):
        for dirn in range(2):
            cols = columns(2 * j + dirn)
            ring(2, dirn, j).wait_recv()
            branch = recvs[2, dirn, j].astype(F32) + part[dirn, j, y]
            gate_row = gate[pl.ds(level, 1), cols]
            done[:, cols] = (lat[:, cols].astype(F32) + gate_row * branch).astype(BF16)
            final(2 * j + dirn).start()

    def tick(tau, carry):
        @pl.when(tau >= 3 * LAG)
        def _():
            last(tau - 3 * LAG)

        for hop in (2, 1):
            @pl.when((tau >= hop * LAG) & (tau < NC + hop * LAG))
            def _(hop=hop):
                middle(hop, tau - hop * LAG)

        @pl.when(tau < NC)
        def _():
            first(tau)

        @pl.when((tau < 6) & (tau % 2 == 1))
        def _():
            w_hand_over(tau + 1)
            w_hand_over(tau + 2)

        return carry

    lax.fori_loop(0, NC + 3 * LAG, tick, 0)

    for d in range(1, SEQ):
        kv_copy(d).wait_send()
        q_copy(d).wait_send()

    def drain_plane(t, carry):
        @pl.when((z == 1) | ((z % 2 == 0) & (t == 0)))
        def _():
            z_copy(t).wait_send()

        for right in range(2):
            x_copy(t, right).wait_send()
            relay(t, right).wait_send()
        return carry

    @pl.when(z == 1)
    def _():
        down_copy().wait_send()

    @pl.when(z == 0)
    def _():
        for copy in mate_part(True, mate) + mate_part(False, z_next(-1)):
            copy.wait_send()

    @pl.when(z == 3)
    def _():
        q_mate.wait_send()

    def drain_sib(n, carry):
        sib_copy(n).wait_send()
        return carry

    for b in range(2):
        @pl.when(z % 3 == 0)
        def _(b=b):
            w_edge(b).wait_send()
            w_inward(b).wait_send()

        for way in range(3):
            w_beside(b, way).wait_send()
    for b in range(8):
        w_sib(b).wait_send()

    def drain_ring(j, carry):
        for dirn in range(2):
            for hop in range(3):
                ring(hop, dirn, j).wait_send()
            final(2 * j + dirn).wait()
        return carry

    lax.fori_loop(0, planes, drain_plane, 0)
    lax.fori_loop(0, 4 * planes, drain_sib, 0)
    lax.fori_loop(0, NC, drain_ring, 0)


def fused(queries, keys_values, mask, level, own, latents, gate_table):
    vmem = pl.BlockSpec(memory_space=pltpu.VMEM)
    anywhere = pl.BlockSpec(memory_space=pl.ANY)
    dma = pltpu.SemaphoreType.DMA
    return pl.pallas_call(
        kernel,
        out_shape=jax.ShapeDtypeStruct((ROWS, D), BF16),
        in_specs=[vmem, vmem] + [anywhere] * 5,
        out_specs=anywhere,
        scratch_shapes=[
            pltpu.VMEM((SEQ, GROUP, ROWS, HD), BF16),
            pltpu.VMEM((SEQ, ROWS, 2 * HD), BF16),
            pltpu.SMEM((32, 32), jnp.int32),
            pltpu.SMEM((32,), jnp.int32),
            pltpu.VMEM((SEQ, GROUP, ROWS, HD), BF16),
            pltpu.VMEM((SEQ, GROUP, ROWS, HD), BF16),
            pltpu.VMEM((2, 4, GROUP, ROWS, HD), BF16),
            pltpu.VMEM((SEQ, GROUP, ROWS, HD), F32),
            pltpu.VMEM((8, QROWS), F32),
            pltpu.VMEM((8, QROWS), F32),
            pltpu.VMEM((2, 8, QROWS), F32),
            pltpu.VMEM((SEQ, ROWS, 2 * HD), BF16),
            pltpu.VMEM((SEQ, GROUP, ROWS, HD), BF16),
            pltpu.VMEM((HD, QROWS), BF16),
            pltpu.VMEM((32, 2 * CT, HD), BF16),
            pltpu.VMEM((HD, QROWS), F32),
            pltpu.VMEM((1, QROWS), F32),
            pltpu.VMEM((1, QROWS), F32),
            pltpu.VMEM((SEQ, GROUP, ROWS, HD), BF16),
            pltpu.VMEM((4, GROUP, ROWS, HD), BF16),
            pltpu.VMEM((2, 4 * ROWS, CT), BF16),
            pltpu.VMEM((BLOCKS, CT, CT), BF16),
            pltpu.VMEM((BLOCKS, CT, CT), BF16),
            pltpu.VMEM((2, NC, 4, ROWS, CT), F32),
            pltpu.VMEM((3, 2, NC, ROWS, CT), BF16),
            pltpu.VMEM((3, 2, NC, ROWS, CT), BF16),
            pltpu.VMEM((ROWS, D), BF16),
            pltpu.VMEM((64, D), F32),
            pltpu.VMEM((ROWS, D), BF16),
            dma((6,)), dma((6,)), dma((SEQ,)), dma((SEQ,)), dma((SEQ,)), dma((SEQ,)),
            dma((4,)), dma((1,)), dma((4, 2)), dma((4, 2)), dma((16,)), dma((32,)), dma((4, 2)),
            dma((BLOCKS + 4,)), dma((2,)), dma((2, 4)), dma((8,)), dma((BLOCKS,)), dma((2,)),
            dma((3, 2, NC)), dma((3, 2, NC)), dma((BLOCKS,)), dma((BLOCKS,)),
        ],
        compiler_params=pltpu.CompilerParams(
            collective_id=0, has_side_effects=True, vmem_limit_bytes=60 * MIB
        ),
        cost_estimate=pl.CostEstimate(
            flops=4 * QROWS * HD * CT * 24, bytes_accessed=20 * MIB, transcendentals=QROWS * CT * 24
        ),
        name="stretch_attention",
    )(queries, keys_values, mask, level, own, latents, gate_table)


def on_device(queries, keys_values, out_weight, latents, gate_table, noise_level, stretch_mask):
    return fused(queries, keys_values, stretch_mask, noise_level, out_weight, latents, gate_table)


def solution(mesh):
    rows = P(("stretch", "seq"), None)
    heads = P(("stretch", "seq"), None, None)
    return jax.shard_map(
        on_device,
        mesh=mesh,
        in_specs=(heads, heads, P("seq", None), rows, P(), P(), P()),
        out_specs=rows,
        check_vma=False,
    )
```

```python
import math

import jax
import jax.numpy as jnp
from jax import lax
from jax.experimental import pallas as pl
from jax.experimental.pallas import tpu as pltpu
from jax.sharding import PartitionSpec as P

MESH = pl.DeviceIdType.MESH
BIG = 1e30
MIB = 2**20
F32, BF16 = jnp.float32, jnp.bfloat16

ROWS = 48
CT = 384
HD = 128
GROUP = 3
SEQ = 8
QROWS = CT * GROUP
D = 6144
EXP_SCALE = math.log2(math.e) / math.sqrt(HD)

NC = 8
BLOCKS = 16


def kernel(
    q_raw, kv_raw, mask_hbm, level_hbm, own_hbm, lat_hbm, gate_hbm, out_ref,
    q_ref, kv_ref, mask_ref, level_ref, q_far, att_far, mate_att, blend, lse, lse_partner, lse_mate, kvr, qr, qt, slots, acc, run_max, run_sum, att, att_in, rows_in,
    own_w, other_w, part, sends, recvs, lat, gate, done,
    mate_send, mate_recv, kv_send, kv_recv, q_send, q_recv, z_send, down_send, x_send, relay_send, sib_send, slot_recv, half_recv,
    load_sem, w_edge_send, w_send, w_sib_send, w_recv, swap_sem, ring_send, ring_recv, out_send, out_recv,
):
    c = lax.axis_index("stretch")
    s = lax.axis_index("seq")
    z, x, k = c // 8, (c // 2) % 4, c % 2
    zh, y = s // 4, s % 4
    bottom = 1 - (z + 3) // 4
    planes = 2 + z // 2 - z // 3

    def dev(zz, xx, kk):
        return ((zz * 4 + xx) * 2 + kk, s)

    def z_next(step):
        pos = (zh * 4 + z + step + 8) % 8
        return (((pos % 4) * 4 + x) * 2 + k, (pos // 4) * 4 + y)

    sibling = dev(z, x, 1 - k)
    above = z_next(1)
    outward = 2 * (z // 3) - 1
    mate = dev(3 - z, x, k)
    x_right, x_left = dev(z, (x + 1) % 4, k), dev(z, (x + 3) % 4, k)
    partner = (c, (s + 4) % SEQ)
    y_up, y_down = (c, zh * 4 + (y + 1) % 4), (c, zh * 4 + (y + 3) % 4)
    after, before = ((c + 1) % 32, s), ((c + 31) % 32, s)

    def push(src, dst, send, recv, target):
        return pltpu.make_async_remote_copy(
            src_ref=src, dst_ref=dst, send_sem=send, recv_sem=recv, device_id=target, device_id_type=MESH
        )

    def load_own(b):
        return pltpu.make_async_copy(own_hbm.at[:, pl.ds(b * CT, CT)], own_w.at[b], load_sem.at[b])

    load_lat = pltpu.make_async_copy(lat_hbm, lat, load_sem.at[BLOCKS])
    load_gate = pltpu.make_async_copy(gate_hbm, gate, load_sem.at[BLOCKS + 1])
    load_mask = pltpu.make_async_copy(mask_hbm, mask_ref, load_sem.at[BLOCKS + 2])
    load_level = pltpu.make_async_copy(level_hbm, level_ref, load_sem.at[BLOCKS + 3])

    barrier = pltpu.get_barrier_semaphore()
    greeted = [(c, (s + d) % SEQ) for d in range(1, SEQ)] + [
        z_next(1), z_next(-1), x_right, x_left, sibling, mate, after, before,
    ]
    for target in greeted:
        pl.semaphore_signal(barrier, inc=1, device_id=target, device_id_type=MESH)
    load_mask.start()
    load_level.start()
    for b in range(BLOCKS):
        load_own(b).start()
    load_lat.start()
    load_gate.start()
    kv_ref[...] = jnp.transpose(kv_raw[...], (1, 0, 2))
    q_ref[...] = jnp.transpose(q_raw[...], (1, 0, 2)).reshape(SEQ, GROUP, ROWS, HD)
    run_max[...] = jnp.full_like(run_max, -BIG)
    run_sum[...] = jnp.zeros_like(run_sum)
    acc[...] = jnp.zeros_like(acc)
    kvr[s] = kv_ref[s]
    qr[s] = q_ref[s]
    pl.semaphore_wait(barrier, len(greeted))

    def kv_copy(d):
        other = (s + d) % SEQ
        return push(kv_ref.at[other], kvr.at[s], kv_send.at[d], kv_recv.at[s], (c, other))

    def q_copy(d):
        other = (s + d) % SEQ
        return push(q_ref.at[other], qr.at[s], q_send.at[d], q_recv.at[s], (c, other))

    def landed(ref, recv, index):
        push(ref.at[index], ref.at[index], kv_send.at[0], recv.at[index], partner).wait_recv()

    for d in (4, 3, 5, 2, 6, 1, 7):
        kv_copy(d).start()
    def block_of(place):
        group = place // 4
        step = group + group // 2 - 2 * (group // 3)
        return 4 * ((x + step) % 4) + place % 4

    def w_push(source, b, send, target):
        return push(source.at[b], other_w.at[b], send, w_recv.at[b], target)

    def core_block(b):
        return block_of(4 * (b // 2) + 2 * k + b % 2)

    def w_edge(b):
        q = core_block(b)
        return push(own_hbm.at[:, pl.ds(pl.multiple_of(q * CT, CT), CT)], other_w.at[q], w_edge_send.at[b], w_recv.at[q], z_next(outward))

    def w_inward(b):
        return w_push(other_w, core_block(b), w_send.at[b, 0], z_next(-outward))

    def w_beside(b, way):
        target = (x_right, x_left)[way]
        return w_push(other_w, core_block(b), w_send.at[b, 1 + way], target)

    def w_across(half):
        moved = core_block(2 * (2 - half) + half)
        return w_push(other_w, moved, w_send.at[half, 3], x_left if half else x_right)

    def w_sib(b):
        return w_push(other_w, core_block(b), w_sib_send.at[b], sibling)

    def w_wait(b):
        w_push(other_w, b, w_sib_send.at[0], sibling).wait_recv()

    def w_spread(b):
        w_wait(core_block(b))

        @pl.when(z % 3 == 0)
        def _():
            w_inward(b).start()

        for way in range(2):
            w_beside(b, way).start()
        w_sib(b).start()

    def w_hand_over(b):
        w_wait(core_block(b))
        w_sib(b).start()

    @pl.when(z % 3 == 0)
    def _():
        for b in range(2):
            w_edge(b).start()

    for d in (4, 3, 5, 2, 6, 1, 7):
        kv_copy(d).wait_send()
    for d in (4, 3, 5, 2, 6, 1, 7):
        q_copy(d).start()
    for d in range(1, SEQ):
        landed(kvr, kv_recv, (s + d) % SEQ)
    block = kvr[...].reshape(CT, 2 * HD)
    slots[c, 0:CT, :] = block[:, :HD]
    value_t = jnp.transpose(block[:, HD:].astype(F32)).astype(BF16)
    for t in range(3):
        slots[c, CT + t * HD : CT + (t + 1) * HD, :] = value_t[:, t * HD : (t + 1) * HD]

    def slot_push(j, send, target):
        return push(slots.at[j], slots.at[j], send, slot_recv.at[j], target)

    def plane_of(t):
        return z - t + 2 * t * bottom

    def column_slot(t):
        return (plane_of(t) * 4 + x) * 2 + k

    def z_copy(t):
        return slot_push(column_slot(t), z_send.at[t], above)

    def x_copy(t, right):
        return slot_push(column_slot(t), x_send.at[t, right], x_right if right else x_left)

    def pair_of(n):
        t, i = n // 4, n % 4
        step = i + i // 2 - 2 * (i // 3)
        return plane_of(t) * 4 + (x + step) % 4

    def sib_copy(n):
        return slot_push(2 * pair_of(n) + k, sib_send.at[n], sibling)

    def half_of(t, pair, right):
        part_of = slots.at[2 * pair + k, pl.ds(CT * right, CT)]
        return push(
            part_of, part_of, relay_send.at[t, right], half_recv.at[t, right], x_right if right else x_left
        )

    def relay(t, right):
        return half_of(t, plane_of(t) * 4 + (x + 1 + 2 * right) % 4, right)

    def wait_slot(j):
        slot_push(j, z_send.at[0], sibling).wait_recv()

    def down_copy():
        return slot_push(column_slot(0), down_send.at[0], z_next(-1))

    def spread(t):
        @pl.when((z == 1) | ((z % 2 == 0) & (t == 0)))
        def _():
            z_copy(t).start()

        @pl.when((z == 1) & (t == 0))
        def _():
            down_copy().start()

        x_copy(t, 0).start()
        x_copy(t, 1).start()
        sib_copy(4 * t).start()

    def from_beside(t, right):
        n = 4 * t + 1 + right
        wait_slot(2 * pair_of(n) + k)
        relay(t, right).start()
        sib_copy(n).start()

    def from_across(t):
        n = 4 * t + 3
        for right in range(2):
            half_of(t, pair_of(n), right).wait_recv()
        sib_copy(n).start()

    def pass_on(t):
        wait_slot(column_slot(t))
        spread(t)

    spread(0)
    from_beside(0, 0)
    from_beside(0, 1)

    pass_on(1)

    for d in range(1, SEQ):
        landed(qr, q_recv, (s + d) % SEQ)
    q_mate = push(qr, q_far, mate_send.at[0], mate_recv.at[0], mate)

    @pl.when(z == 3)
    def _():
        q_mate.start()

    def take_queries(source):
        qt[...] = jnp.transpose(source[...].reshape(QROWS, HD).astype(F32)).astype(BF16)

    take_queries(qr)
    for b in range(BLOCKS):
        load_own(b).wait()


    load_mask.wait()
    load_level.wait()

    own_pair = z * 4 + x
    swap = push(att.at[pl.ds(4 * (1 - zh), 4)], att_in, swap_sem.at[0], swap_sem.at[1], partner)
    lse_swap = push(lse, lse_partner, mate_send.at[1], mate_recv.at[1], partner)

    def mate_part(near, target):
        half = zh if near else 1 - zh
        at = 0 if near else 1
        return (
            push(att_far.at[pl.ds(4 * half, 4)], mate_att.at[at], mate_send.at[2 + at], mate_recv.at[2 + at], target),
            push(lse, lse_mate.at[at], mate_send.at[4 + at], mate_recv.at[4 + at], target),
        )

    def finish(target):
        total_weight = jnp.maximum(run_sum[...], 1e-30)
        out = jnp.transpose(acc[...] * (1.0 / total_weight)).astype(BF16)
        target[...] = out.reshape(SEQ, GROUP, ROWS, HD)
        lse[...] = jnp.broadcast_to(run_max[...] * EXP_SCALE + jnp.log2(total_weight), lse.shape)

    def attend(pair, row):
        ja = 2 * pair
        hide_a = jnp.where(mask_ref[row, ja] == 1, 0.0, 2 * BIG).astype(F32)
        hide_b = jnp.where(mask_ref[row, ja + 1] == 1, 0.0, 2 * BIG).astype(F32)
        ones = jnp.ones((16, CT), BF16)

        def values(j):
            cut = [slots[j, CT + t * HD : CT + (t + 1) * HD, :] for t in range(3)]
            return jnp.concatenate([jnp.concatenate(cut, axis=1), ones], axis=0)

        va, vb = values(ja), values(ja + 1)
        ka, kb = slots[ja, 0:CT, :], slots[ja + 1, 0:CT, :]

        def score(r):
            q_cols = qt[:, r * CT : (r + 1) * CT]
            return (
                jnp.dot(ka, q_cols, preferred_element_type=F32),
                jnp.dot(kb, q_cols, preferred_element_type=F32),
            )

        ready = score(0)
        for r in range(GROUP):
            ahead = score(r + 1) if r + 1 < GROUP else None
            sa, sb = ready
            cols = slice(r * CT, (r + 1) * CT)
            top = jnp.maximum(
                jnp.max(sa, axis=0, keepdims=True) - hide_a, jnp.max(sb, axis=0, keepdims=True) - hide_b
            )
            old = run_max[:, cols]
            new = jnp.maximum(old, top)
            factor = jnp.exp2((old - new) * EXP_SCALE)
            pa = jnp.exp2((sa - (new + hide_a)) * EXP_SCALE)
            pb = jnp.exp2((sb - (new + hide_b)) * EXP_SCALE)
            run_max[:, cols] = new
            update = jnp.dot(va, pa.astype(BF16), preferred_element_type=F32) + jnp.dot(
                vb, pb.astype(BF16), preferred_element_type=F32
            )
            run_sum[:, cols] = run_sum[:, cols] * factor + update[HD : HD + 1]
            acc[:, cols] = acc[:, cols] * factor + update[:HD]
            ready = ahead

    w_first = jnp.where(z == 0, 1, jnp.where(z == 1, 4, jnp.where(z == 2, 8, 1)))
    w_count = 2

    def step(n, carry):
        t, i = (n // 4) // (1 + bottom), n % 4
        fresh = (bottom == 0) | (n // 4 != 1)
        for_mate = (bottom == 1) & (n >= 4)
        pair = pair_of(4 * t + i)

        @pl.when((bottom == 1) & (n == 4))
        def _():
            finish(att)
            swap.start()
            q_mate.wait_recv()
            take_queries(q_far)
            run_max[...] = jnp.full_like(run_max, -BIG)
            run_sum[...] = jnp.zeros_like(run_sum)
            acc[...] = jnp.zeros_like(acc)

        @pl.when(fresh)
        def _():
            wait_slot(2 * pair + 1 - k)

        @pl.when((pair <= own_pair) | for_mate)
        def _():
            attend(pair, c + 24 * bottom * ((n + 8) // 12))

        @pl.when((n == 1) & (z == 2))
        def _():
            pass_on(2)

        @pl.when((i == 1) & fresh)
        def _():
            from_across(t)

        @pl.when((i == 3) & (n // 4 + 1 < planes))
        def _():
            from_beside(n // 4 + 1, 0)
            from_beside(n // 4 + 1, 1)

        turn = n - w_first

        @pl.when((turn >= 0) & (turn % 3 == 0) & (turn < 3 * w_count))
        def _():
            w_spread(turn // 3)

        return carry

    lax.fori_loop(0, 4 * (planes + bottom), step, 0)

    @pl.when(z == 0)
    def _():
        finish(att_far)
        for copy in mate_part(True, mate) + mate_part(False, z_next(-1)):
            copy.start()

    @pl.when(z != 0)
    def _():
        finish(att)
        swap.start()

    @pl.when(z == 3)
    def _():
        lse_swap.start()

    def gather_rows(source, first, place):
        for h in range(GROUP):
            rows_in[place, :, h * HD : (h + 1) * HD] = source[pl.ds(first, 4), h].reshape(4 * ROWS, HD)

    def blended(near, lse_home, lse_far, home, far):
        top = jnp.maximum(lse_home, lse_far)
        home_weight, far_weight = jnp.exp2(lse_home - top), jnp.exp2(lse_far - top)
        share = jnp.broadcast_to(home_weight / (home_weight + far_weight), (HD, QROWS))
        blend[...] = jnp.transpose(share).reshape(SEQ, GROUP, ROWS, HD)
        part_of = blend[pl.ds(4 * zh, 4)]
        mixed = part_of * home.astype(F32) + (1.0 - part_of) * far.astype(F32)
        return mixed.astype(BF16)

    for group in (1, 2):
        for half in range(2):
            w_hand_over(2 * group + half)
        w_across(2 - group).start()
    swap.wait()

    @pl.when(z == 3)
    def _():
        lse_swap.wait()
        for copy in mate_part(True, mate) + mate_part(False, mate):
            copy.wait_recv()
        att[pl.ds(4 * zh, 4)] = blended(True, lse[0:1], lse_mate[0, 0:1], att[pl.ds(4 * zh, 4)], mate_att[0])
        att_in[...] = blended(False, lse_partner[0:1], lse_mate[1, 0:1], att_in[...], mate_att[1])

    gather_rows(att, 4 * zh, 0)
    gather_rows(att_in, 0, 1)

    def ring(hop, dirn, j):
        return push(
            sends.at[hop, dirn, j], recvs.at[hop, dirn, j],
            ring_send.at[hop, dirn, j], ring_recv.at[hop, dirn, j], y_down if dirn else y_up,
        )

    def block_at(hop, dirn):
        return (y + 1 + hop) % 4 if dirn else (y + 3 - hop) % 4

    def columns(place):
        return pl.ds(pl.multiple_of(block_of(place) * CT, CT), CT)

    def final(place):
        cols = columns(place)
        return push(done.at[:, cols], out_ref.at[:, cols], out_send.at[place], out_recv.at[place], after)

    load_lat.wait()
    load_gate.wait()
    level = level_ref[c]

    def first(j):
        @pl.when(j % 2 != k)
        def _():
            for dirn in range(2):
                w_wait(block_of(2 * j + dirn))

        for dirn in range(2):
            q = block_of(2 * j + dirn)
            product = jnp.dot(rows_in[0], own_w[q], preferred_element_type=F32)
            product += jnp.dot(rows_in[1], other_w[q], preferred_element_type=F32)
            part[dirn, j] = product.reshape(4, ROWS, CT)
            sends[0, dirn, j] = part[dirn, j, block_at(0, dirn)].astype(BF16)
            ring(0, dirn, j).start()

    def middle(hop, j):
        for dirn in range(2):
            ring(hop - 1, dirn, j).wait_recv()
            sends[hop, dirn, j] = (
                recvs[hop - 1, dirn, j].astype(F32) + part[dirn, j, block_at(hop, dirn)]
            ).astype(BF16)
            ring(hop, dirn, j).start()

    def last(j):
        for dirn in range(2):
            cols = columns(2 * j + dirn)
            ring(2, dirn, j).wait_recv()
            branch = recvs[2, dirn, j].astype(F32) + part[dirn, j, y]
            gate_row = gate[pl.ds(level, 1), cols]
            done[:, cols] = (lat[:, cols].astype(F32) + gate_row * branch).astype(BF16)
            final(2 * j + dirn).start()

    def run(lo, hi, work):
        def body(j, carry):
            work(j)
            return carry

        lax.fori_loop(lo, hi, body, 0)

    early, late = NC // 2, NC
    run(0, early, first)
    run(0, early, lambda j: middle(1, j))
    run(early, early + 2, first)
    run(0, early, lambda j: middle(2, j))
    w_hand_over(6)
    w_hand_over(7)
    run(early + 2, late, first)
    run(early, late, lambda j: middle(1, j))
    run(0, early, last)
    run(early, late, lambda j: middle(2, j))
    run(early, late, last)

    for d in range(1, SEQ):
        q_copy(d).wait_send()

    def drain_plane(t, carry):
        @pl.when((z == 1) | ((z % 2 == 0) & (t == 0)))
        def _():
            z_copy(t).wait_send()

        for right in range(2):
            x_copy(t, right).wait_send()
            relay(t, right).wait_send()
        return carry

    @pl.when(z == 1)
    def _():
        down_copy().wait_send()

    @pl.when(z == 0)
    def _():
        for copy in mate_part(True, mate) + mate_part(False, z_next(-1)):
            copy.wait_send()

    @pl.when(z == 3)
    def _():
        q_mate.wait_send()

    def drain_sib(n, carry):
        sib_copy(n).wait_send()
        return carry

    for b in range(2):
        @pl.when(z % 3 == 0)
        def _(b=b):
            w_edge(b).wait_send()
            w_inward(b).wait_send()

        for way in range(2):
            w_beside(b, way).wait_send()
        w_across(b).wait_send()
    for b in range(8):
        w_sib(b).wait_send()

    def drain_ring(j, carry):
        for dirn in range(2):
            for hop in range(3):
                ring(hop, dirn, j).wait_send()
            final(2 * j + dirn).wait()
        return carry

    lax.fori_loop(0, planes, drain_plane, 0)
    lax.fori_loop(0, 4 * planes, drain_sib, 0)
    lax.fori_loop(0, NC, drain_ring, 0)


def fused(queries, keys_values, mask, level, own, latents, gate_table):
    vmem = pl.BlockSpec(memory_space=pltpu.VMEM)
    anywhere = pl.BlockSpec(memory_space=pl.ANY)
    dma = pltpu.SemaphoreType.DMA
    return pl.pallas_call(
        kernel,
        out_shape=jax.ShapeDtypeStruct((ROWS, D), BF16),
        in_specs=[vmem, vmem] + [anywhere] * 5,
        out_specs=anywhere,
        scratch_shapes=[
            pltpu.VMEM((SEQ, GROUP, ROWS, HD), BF16),
            pltpu.VMEM((SEQ, ROWS, 2 * HD), BF16),
            pltpu.SMEM((32, 32), jnp.int32),
            pltpu.SMEM((32,), jnp.int32),
            pltpu.VMEM((SEQ, GROUP, ROWS, HD), BF16),
            pltpu.VMEM((SEQ, GROUP, ROWS, HD), BF16),
            pltpu.VMEM((2, 4, GROUP, ROWS, HD), BF16),
            pltpu.VMEM((SEQ, GROUP, ROWS, HD), F32),
            pltpu.VMEM((8, QROWS), F32),
            pltpu.VMEM((8, QROWS), F32),
            pltpu.VMEM((2, 8, QROWS), F32),
            pltpu.VMEM((SEQ, ROWS, 2 * HD), BF16),
            pltpu.VMEM((SEQ, GROUP, ROWS, HD), BF16),
            pltpu.VMEM((HD, QROWS), BF16),
            pltpu.VMEM((32, 2 * CT, HD), BF16),
            pltpu.VMEM((HD, QROWS), F32),
            pltpu.VMEM((1, QROWS), F32),
            pltpu.VMEM((1, QROWS), F32),
            pltpu.VMEM((SEQ, GROUP, ROWS, HD), BF16),
            pltpu.VMEM((4, GROUP, ROWS, HD), BF16),
            pltpu.VMEM((2, 4 * ROWS, CT), BF16),
            pltpu.VMEM((BLOCKS, CT, CT), BF16),
            pltpu.VMEM((BLOCKS, CT, CT), BF16),
            pltpu.VMEM((2, NC, 4, ROWS, CT), F32),
            pltpu.VMEM((3, 2, NC, ROWS, CT), BF16),
            pltpu.VMEM((3, 2, NC, ROWS, CT), BF16),
            pltpu.VMEM((ROWS, D), BF16),
            pltpu.VMEM((64, D), F32),
            pltpu.VMEM((ROWS, D), BF16),
            dma((6,)), dma((6,)), dma((SEQ,)), dma((SEQ,)), dma((SEQ,)), dma((SEQ,)),
            dma((4,)), dma((1,)), dma((4, 2)), dma((4, 2)), dma((16,)), dma((32,)), dma((4, 2)),
            dma((BLOCKS + 4,)), dma((2,)), dma((2, 4)), dma((8,)), dma((BLOCKS,)), dma((2,)),
            dma((3, 2, NC)), dma((3, 2, NC)), dma((BLOCKS,)), dma((BLOCKS,)),
        ],
        compiler_params=pltpu.CompilerParams(
            collective_id=0, has_side_effects=True, vmem_limit_bytes=60 * MIB
        ),
        cost_estimate=pl.CostEstimate(
            flops=4 * QROWS * HD * CT * 24, bytes_accessed=20 * MIB, transcendentals=QROWS * CT * 24
        ),
        name="stretch_attention",
    )(queries, keys_values, mask, level, own, latents, gate_table)


def on_device(queries, keys_values, out_weight, latents, gate_table, noise_level, stretch_mask):
    return fused(queries, keys_values, stretch_mask, noise_level, out_weight, latents, gate_table)


def solution(mesh):
    rows = P(("stretch", "seq"), None)
    heads = P(("stretch", "seq"), None, None)
    return jax.shard_map(
        on_device,
        mesh=mesh,
        in_specs=(heads, heads, P("seq", None), rows, P(), P(), P()),
        out_specs=rows,
        check_vma=False,
    )
```

```python
import math

import jax
import jax.numpy as jnp
from jax import lax
from jax.experimental import pallas as pl
from jax.experimental.pallas import tpu as pltpu
from jax.sharding import PartitionSpec as P

MESH = pl.DeviceIdType.MESH
BIG = 1e30
MIB = 2**20
F32, BF16 = jnp.float32, jnp.bfloat16

ROWS = 48
CT = 384
HD = 128
GROUP = 3
SEQ = 8
QROWS = CT * GROUP
D = 6144
EXP_SCALE = math.log2(math.e) / math.sqrt(HD)

NC = 8
BLOCKS = 16


def kernel(
    q_raw, kv_raw, mask_hbm, level_hbm, own_hbm, lat_hbm, gate_hbm, out_ref,
    q_ref, kv_ref, mask_ref, level_ref, q_far, att_far, mate_att, blend, lse, lse_partner, lse_mate, kvr, qr, qt, slots, acc, run_max, run_sum, att, att_in, rows_in,
    own_w, other_w, part, sends, recvs, lat, gate, done,
    mate_send, mate_recv, kv_send, kv_recv, q_send, q_recv, z_send, down_send, x_send, relay_send, sib_send, slot_recv, half_recv,
    load_sem, w_edge_send, w_send, w_sib_send, w_recv, swap_sem, ring_send, ring_recv, out_send, out_recv,
):
    c = lax.axis_index("stretch")
    s = lax.axis_index("seq")
    z, x, k = c // 8, (c // 2) % 4, c % 2
    zh, y = s // 4, s % 4
    bottom = 1 - (z + 3) // 4
    planes = 2 + z // 2 - z // 3

    def dev(zz, xx, kk):
        return ((zz * 4 + xx) * 2 + kk, s)

    def z_next(step):
        pos = (zh * 4 + z + step + 8) % 8
        return (((pos % 4) * 4 + x) * 2 + k, (pos // 4) * 4 + y)

    sibling = dev(z, x, 1 - k)
    above = z_next(1)
    outward = 2 * (z // 3) - 1
    mate = dev(3 - z, x, k)
    x_right, x_left = dev(z, (x + 1) % 4, k), dev(z, (x + 3) % 4, k)
    partner = (c, (s + 4) % SEQ)
    y_up, y_down = (c, zh * 4 + (y + 1) % 4), (c, zh * 4 + (y + 3) % 4)
    after, before = ((c + 1) % 32, s), ((c + 31) % 32, s)

    def push(src, dst, send, recv, target):
        return pltpu.make_async_remote_copy(
            src_ref=src, dst_ref=dst, send_sem=send, recv_sem=recv, device_id=target, device_id_type=MESH
        )

    def load_own(b):
        return pltpu.make_async_copy(own_hbm.at[:, pl.ds(b * CT, CT)], own_w.at[b], load_sem.at[b])

    load_lat = pltpu.make_async_copy(lat_hbm, lat, load_sem.at[BLOCKS])
    load_gate = pltpu.make_async_copy(gate_hbm, gate, load_sem.at[BLOCKS + 1])
    load_mask = pltpu.make_async_copy(mask_hbm, mask_ref, load_sem.at[BLOCKS + 2])
    load_level = pltpu.make_async_copy(level_hbm, level_ref, load_sem.at[BLOCKS + 3])

    barrier = pltpu.get_barrier_semaphore()
    greeted = [(c, (s + d) % SEQ) for d in range(1, SEQ)] + [
        z_next(1), z_next(-1), x_right, x_left, sibling, mate, after, before,
    ]
    for target in greeted:
        pl.semaphore_signal(barrier, inc=1, device_id=target, device_id_type=MESH)
    load_mask.start()
    load_level.start()
    for b in range(BLOCKS):
        load_own(b).start()
    load_lat.start()
    load_gate.start()
    kv_ref[...] = jnp.transpose(kv_raw[...], (1, 0, 2))
    q_ref[...] = jnp.transpose(q_raw[...], (1, 0, 2)).reshape(SEQ, GROUP, ROWS, HD)
    run_max[...] = jnp.full_like(run_max, -BIG)
    run_sum[...] = jnp.zeros_like(run_sum)
    acc[...] = jnp.zeros_like(acc)
    kvr[s] = kv_ref[s]
    qr[s] = q_ref[s]
    pl.semaphore_wait(barrier, len(greeted))

    def kv_copy(d):
        other = (s + d) % SEQ
        return push(kv_ref.at[other], kvr.at[s], kv_send.at[d], kv_recv.at[s], (c, other))

    def q_copy(d):
        other = (s + d) % SEQ
        return push(q_ref.at[other], qr.at[s], q_send.at[d], q_recv.at[s], (c, other))

    def landed(ref, recv, index):
        push(ref.at[index], ref.at[index], kv_send.at[0], recv.at[index], partner).wait_recv()

    for d in (4, 3, 5, 2, 6, 1, 7):
        kv_copy(d).start()
    def block_of(place):
        group = place // 4
        step = group + group // 2 - 2 * (group // 3)
        return 4 * ((x + step) % 4) + place % 4

    def w_push(source, b, send, target):
        return push(source.at[b], other_w.at[b], send, w_recv.at[b], target)

    def core_block(b):
        return block_of(4 * (b // 2) + 2 * k + b % 2)

    def w_edge(b):
        q = core_block(b)
        return push(own_hbm.at[:, pl.ds(pl.multiple_of(q * CT, CT), CT)], other_w.at[q], w_edge_send.at[b], w_recv.at[q], z_next(outward))

    def w_inward(b):
        return w_push(other_w, core_block(b), w_send.at[b, 0], z_next(-outward))

    def w_beside(b, way):
        target = (x_right, x_left)[way]
        return w_push(other_w, core_block(b), w_send.at[b, 1 + way], target)

    def w_across(half):
        moved = core_block(2 * (2 - half) + half)
        return w_push(other_w, moved, w_send.at[half, 3], x_left if half else x_right)

    def w_sib(b):
        return w_push(other_w, core_block(b), w_sib_send.at[b], sibling)

    def w_wait(b):
        w_push(other_w, b, w_sib_send.at[0], sibling).wait_recv()

    def w_spread(b):
        w_wait(core_block(b))

        @pl.when(z % 3 == 0)
        def _():
            w_inward(b).start()

        for way in range(2):
            w_beside(b, way).start()
        w_sib(b).start()

    def w_hand_over(b):
        w_wait(core_block(b))
        w_sib(b).start()

    @pl.when(z % 3 == 0)
    def _():
        for b in range(2):
            w_edge(b).start()

    for d in (4, 3, 5, 2, 6, 1, 7):
        kv_copy(d).wait_send()
    for d in (4, 3, 5, 2, 6, 1, 7):
        q_copy(d).start()
    for d in range(1, SEQ):
        landed(kvr, kv_recv, (s + d) % SEQ)
    block = kvr[...].reshape(CT, 2 * HD)
    slots[c, 0:CT, :] = block[:, :HD]
    value_t = jnp.transpose(block[:, HD:].astype(F32)).astype(BF16)
    for t in range(3):
        slots[c, CT + t * HD : CT + (t + 1) * HD, :] = value_t[:, t * HD : (t + 1) * HD]

    def slot_push(j, send, target):
        return push(slots.at[j], slots.at[j], send, slot_recv.at[j], target)

    def plane_of(t):
        return z - t + 2 * t * bottom

    def column_slot(t):
        return (plane_of(t) * 4 + x) * 2 + k

    def z_copy(t):
        return slot_push(column_slot(t), z_send.at[t], above)

    def x_copy(t, right):
        return slot_push(column_slot(t), x_send.at[t, right], x_right if right else x_left)

    def pair_of(n):
        t, i = n // 4, n % 4
        step = i + i // 2 - 2 * (i // 3)
        return plane_of(t) * 4 + (x + step) % 4

    def sib_copy(n):
        return slot_push(2 * pair_of(n) + k, sib_send.at[n], sibling)

    def half_of(t, pair, right):
        part_of = slots.at[2 * pair + k, pl.ds(CT * right, CT)]
        return push(
            part_of, part_of, relay_send.at[t, right], half_recv.at[t, right], x_right if right else x_left
        )

    def relay(t, right):
        return half_of(t, plane_of(t) * 4 + (x + 1 + 2 * right) % 4, right)

    def wait_slot(j):
        slot_push(j, z_send.at[0], sibling).wait_recv()

    def down_copy():
        return slot_push(column_slot(0), down_send.at[0], z_next(-1))

    def spread(t):
        @pl.when((z == 1) | ((z % 2 == 0) & (t == 0)))
        def _():
            z_copy(t).start()

        @pl.when((z == 1) & (t == 0))
        def _():
            down_copy().start()

        x_copy(t, 0).start()
        x_copy(t, 1).start()
        sib_copy(4 * t).start()

    def from_beside(t, right):
        n = 4 * t + 1 + right
        wait_slot(2 * pair_of(n) + k)
        relay(t, right).start()
        sib_copy(n).start()

    def from_across(t):
        n = 4 * t + 3
        for right in range(2):
            half_of(t, pair_of(n), right).wait_recv()
        sib_copy(n).start()

    def pass_on(t):
        wait_slot(column_slot(t))
        spread(t)

    spread(0)
    from_beside(0, 0)
    from_beside(0, 1)

    pass_on(1)

    for d in range(1, SEQ):
        landed(qr, q_recv, (s + d) % SEQ)
    q_mate = push(qr, q_far, mate_send.at[0], mate_recv.at[0], mate)

    @pl.when(z == 3)
    def _():
        q_mate.start()

    def take_queries(source):
        qt[...] = jnp.transpose(source[...].reshape(QROWS, HD).astype(F32)).astype(BF16)

    take_queries(qr)
    for b in range(BLOCKS):
        load_own(b).wait()


    load_mask.wait()
    load_level.wait()

    own_pair = z * 4 + x
    swap = push(att.at[pl.ds(4 * (1 - zh), 4)], att_in, swap_sem.at[0], swap_sem.at[1], partner)
    lse_swap = push(lse, lse_partner, mate_send.at[1], mate_recv.at[1], partner)

    def mate_part(near, target):
        half = zh if near else 1 - zh
        at = 0 if near else 1
        return (
            push(att_far.at[pl.ds(4 * half, 4)], mate_att.at[at], mate_send.at[2 + at], mate_recv.at[2 + at], target),
            push(lse, lse_mate.at[at], mate_send.at[4 + at], mate_recv.at[4 + at], target),
        )

    def finish(target):
        total_weight = jnp.maximum(run_sum[...], 1e-30)
        out = jnp.transpose(acc[...] * (1.0 / total_weight)).astype(BF16)
        target[...] = out.reshape(SEQ, GROUP, ROWS, HD)
        lse[...] = jnp.broadcast_to(run_max[...] * EXP_SCALE + jnp.log2(total_weight), lse.shape)

    def attend(pair, row):
        ja = 2 * pair
        hide_a = jnp.where(mask_ref[row, ja] == 1, 0.0, 2 * BIG).astype(F32)
        hide_b = jnp.where(mask_ref[row, ja + 1] == 1, 0.0, 2 * BIG).astype(F32)
        ones = jnp.ones((16, CT), BF16)

        def values(j):
            cut = [slots[j, CT + t * HD : CT + (t + 1) * HD, :] for t in range(3)]
            return jnp.concatenate([jnp.concatenate(cut, axis=1), ones], axis=0)

        va, vb = values(ja), values(ja + 1)
        ka, kb = slots[ja, 0:CT, :], slots[ja + 1, 0:CT, :]

        def score(r):
            q_cols = qt[:, r * CT : (r + 1) * CT]
            return (
                jnp.dot(ka, q_cols, preferred_element_type=F32),
                jnp.dot(kb, q_cols, preferred_element_type=F32),
            )

        scores = [score(r) for r in range(GROUP)]
        for r in range(GROUP):
            sa, sb = scores[r]
            cols = slice(r * CT, (r + 1) * CT)
            top = jnp.maximum(
                jnp.max(sa, axis=0, keepdims=True) - hide_a, jnp.max(sb, axis=0, keepdims=True) - hide_b
            )
            old = run_max[:, cols]
            new = jnp.maximum(old, top)
            factor = jnp.exp2((old - new) * EXP_SCALE)
            pa = jnp.exp2((sa - (new + hide_a)) * EXP_SCALE)
            pb = jnp.exp2((sb - (new + hide_b)) * EXP_SCALE)
            run_max[:, cols] = new
            update = jnp.dot(va, pa.astype(BF16), preferred_element_type=F32) + jnp.dot(
                vb, pb.astype(BF16), preferred_element_type=F32
            )
            run_sum[:, cols] = run_sum[:, cols] * factor + update[HD : HD + 1]
            acc[:, cols] = acc[:, cols] * factor + update[:HD]

    w_first = jnp.where(z == 0, 1, jnp.where(z == 1, 4, jnp.where(z == 2, 8, 1)))
    w_count = 2

    def step(n, carry):
        t, i = (n // 4) // (1 + bottom), n % 4
        fresh = (bottom == 0) | (n // 4 != 1)
        for_mate = (bottom == 1) & (n >= 4)
        pair = pair_of(4 * t + i)

        @pl.when((bottom == 1) & (n == 4))
        def _():
            finish(att)
            swap.start()
            q_mate.wait_recv()
            take_queries(q_far)
            run_max[...] = jnp.full_like(run_max, -BIG)
            run_sum[...] = jnp.zeros_like(run_sum)
            acc[...] = jnp.zeros_like(acc)

        @pl.when(fresh)
        def _():
            wait_slot(2 * pair + 1 - k)

        @pl.when((pair <= own_pair) | for_mate)
        def _():
            attend(pair, c + 24 * bottom * ((n + 8) // 12))

        @pl.when((n == 1) & (z == 2))
        def _():
            pass_on(2)

        @pl.when((i == 1) & fresh)
        def _():
            from_across(t)

        @pl.when((i == 3) & (n // 4 + 1 < planes))
        def _():
            from_beside(n // 4 + 1, 0)
            from_beside(n // 4 + 1, 1)

        turn = n - w_first

        @pl.when((turn >= 0) & (turn % 2 == 0) & (turn < 2 * w_count))
        def _():
            w_spread(turn // 2)

        return carry

    lax.fori_loop(0, 4 * (planes + bottom), step, 0)

    @pl.when(z == 0)
    def _():
        finish(att_far)
        for copy in mate_part(True, mate) + mate_part(False, z_next(-1)):
            copy.start()

    @pl.when(z != 0)
    def _():
        finish(att)
        swap.start()

    @pl.when(z == 3)
    def _():
        lse_swap.start()

    def gather_rows(source, first, place):
        for h in range(GROUP):
            rows_in[place, :, h * HD : (h + 1) * HD] = source[pl.ds(first, 4), h].reshape(4 * ROWS, HD)

    def blended(near, lse_home, lse_far, home, far):
        top = jnp.maximum(lse_home, lse_far)
        home_weight, far_weight = jnp.exp2(lse_home - top), jnp.exp2(lse_far - top)
        share = jnp.broadcast_to(home_weight / (home_weight + far_weight), (HD, QROWS))
        blend[...] = jnp.transpose(share).reshape(SEQ, GROUP, ROWS, HD)
        part_of = blend[pl.ds(4 * zh, 4)]
        mixed = part_of * home.astype(F32) + (1.0 - part_of) * far.astype(F32)
        return mixed.astype(BF16)

    for group in (1, 2):
        for half in range(2):
            w_hand_over(2 * group + half)
        w_across(2 - group).start()
    swap.wait()

    @pl.when(z == 3)
    def _():
        lse_swap.wait()
        for copy in mate_part(True, mate) + mate_part(False, mate):
            copy.wait_recv()
        att[pl.ds(4 * zh, 4)] = blended(True, lse[0:1], lse_mate[0, 0:1], att[pl.ds(4 * zh, 4)], mate_att[0])
        att_in[...] = blended(False, lse_partner[0:1], lse_mate[1, 0:1], att_in[...], mate_att[1])

    gather_rows(att, 4 * zh, 0)
    gather_rows(att_in, 0, 1)

    def ring(hop, dirn, j):
        target = y_up if (dirn == 0) == (hop < 2) else y_down
        return push(
            sends.at[hop, dirn, j], recvs.at[hop, dirn, j],
            ring_send.at[hop, dirn, j], ring_recv.at[hop, dirn, j], target,
        )

    def columns(place):
        return pl.ds(pl.multiple_of(block_of(place) * CT, CT), CT)

    def final(place):
        cols = columns(place)
        return push(done.at[:, cols], out_ref.at[:, cols], out_send.at[place], out_recv.at[place], after)

    load_lat.wait()
    load_gate.wait()
    level = level_ref[c]

    def first(j):
        @pl.when(j % 2 != k)
        def _():
            for dirn in range(2):
                w_wait(block_of(2 * j + dirn))

        for dirn in range(2):
            q = block_of(2 * j + dirn)
            product = jnp.dot(rows_in[0], own_w[q], preferred_element_type=F32)
            product += jnp.dot(rows_in[1], other_w[q], preferred_element_type=F32)
            part[dirn, j] = product.reshape(4, ROWS, CT)
            sends[0, dirn, j] = part[dirn, j, (y + 2) % 4].astype(BF16)
            ring(0, dirn, j).start()
        for dirn in range(2):
            sends[2, dirn, j] = part[dirn, j, (y + 3 - 2 * dirn) % 4].astype(BF16)
            ring(2, dirn, j).start()

    def middle(j):
        for dirn in range(2):
            ring(0, dirn, j).wait_recv()
            sends[1, dirn, j] = (
                recvs[0, dirn, j].astype(F32) + part[dirn, j, (y + 1 + 2 * dirn) % 4]
            ).astype(BF16)
            ring(1, dirn, j).start()

    def last(j):
        for dirn in range(2):
            cols = columns(2 * j + dirn)
            ring(1, dirn, j).wait_recv()
            ring(2, dirn, j).wait_recv()
            branch = recvs[1, dirn, j].astype(F32) + recvs[2, dirn, j].astype(F32) + part[dirn, j, y]
            gate_row = gate[pl.ds(level, 1), cols]
            done[:, cols] = (lat[:, cols].astype(F32) + gate_row * branch).astype(BF16)
            final(2 * j + dirn).start()

    def run(lo, hi, work):
        def body(j, carry):
            work(j)
            return carry

        lax.fori_loop(lo, hi, body, 0)

    run(0, 4, first)
    run(0, 4, middle)
    run(4, 6, first)
    w_hand_over(6)
    w_hand_over(7)
    run(6, 8, first)
    run(4, 6, middle)
    run(0, 4, last)
    run(6, 8, middle)
    run(4, 8, last)

    for d in range(1, SEQ):
        q_copy(d).wait_send()

    def drain_plane(t, carry):
        @pl.when((z == 1) | ((z % 2 == 0) & (t == 0)))
        def _():
            z_copy(t).wait_send()

        for right in range(2):
            x_copy(t, right).wait_send()
            relay(t, right).wait_send()
        return carry

    @pl.when(z == 1)
    def _():
        down_copy().wait_send()

    @pl.when(z == 0)
    def _():
        for copy in mate_part(True, mate) + mate_part(False, z_next(-1)):
            copy.wait_send()

    @pl.when(z == 3)
    def _():
        q_mate.wait_send()

    def drain_sib(n, carry):
        sib_copy(n).wait_send()
        return carry

    for b in range(2):
        @pl.when(z % 3 == 0)
        def _(b=b):
            w_edge(b).wait_send()
            w_inward(b).wait_send()

        for way in range(2):
            w_beside(b, way).wait_send()
        w_across(b).wait_send()
    for b in range(8):
        w_sib(b).wait_send()

    def drain_ring(j, carry):
        for dirn in range(2):
            for hop in range(3):
                ring(hop, dirn, j).wait_send()
            final(2 * j + dirn).wait()
        return carry

    lax.fori_loop(0, planes, drain_plane, 0)
    lax.fori_loop(0, 4 * planes, drain_sib, 0)
    lax.fori_loop(0, NC, drain_ring, 0)


def fused(queries, keys_values, mask, level, own, latents, gate_table):
    vmem = pl.BlockSpec(memory_space=pltpu.VMEM)
    anywhere = pl.BlockSpec(memory_space=pl.ANY)
    dma = pltpu.SemaphoreType.DMA
    return pl.pallas_call(
        kernel,
        out_shape=jax.ShapeDtypeStruct((ROWS, D), BF16),
        in_specs=[vmem, vmem] + [anywhere] * 5,
        out_specs=anywhere,
        scratch_shapes=[
            pltpu.VMEM((SEQ, GROUP, ROWS, HD), BF16),
            pltpu.VMEM((SEQ, ROWS, 2 * HD), BF16),
            pltpu.SMEM((32, 32), jnp.int32),
            pltpu.SMEM((32,), jnp.int32),
            pltpu.VMEM((SEQ, GROUP, ROWS, HD), BF16),
            pltpu.VMEM((SEQ, GROUP, ROWS, HD), BF16),
            pltpu.VMEM((2, 4, GROUP, ROWS, HD), BF16),
            pltpu.VMEM((SEQ, GROUP, ROWS, HD), F32),
            pltpu.VMEM((8, QROWS), F32),
            pltpu.VMEM((8, QROWS), F32),
            pltpu.VMEM((2, 8, QROWS), F32),
            pltpu.VMEM((SEQ, ROWS, 2 * HD), BF16),
            pltpu.VMEM((SEQ, GROUP, ROWS, HD), BF16),
            pltpu.VMEM((HD, QROWS), BF16),
            pltpu.VMEM((32, 2 * CT, HD), BF16),
            pltpu.VMEM((HD, QROWS), F32),
            pltpu.VMEM((1, QROWS), F32),
            pltpu.VMEM((1, QROWS), F32),
            pltpu.VMEM((SEQ, GROUP, ROWS, HD), BF16),
            pltpu.VMEM((4, GROUP, ROWS, HD), BF16),
            pltpu.VMEM((2, 4 * ROWS, CT), BF16),
            pltpu.VMEM((BLOCKS, CT, CT), BF16),
            pltpu.VMEM((BLOCKS, CT, CT), BF16),
            pltpu.VMEM((2, NC, 4, ROWS, CT), F32),
            pltpu.VMEM((3, 2, NC, ROWS, CT), BF16),
            pltpu.VMEM((3, 2, NC, ROWS, CT), BF16),
            pltpu.VMEM((ROWS, D), BF16),
            pltpu.VMEM((64, D), F32),
            pltpu.VMEM((ROWS, D), BF16),
            dma((6,)), dma((6,)), dma((SEQ,)), dma((SEQ,)), dma((SEQ,)), dma((SEQ,)),
            dma((4,)), dma((1,)), dma((4, 2)), dma((4, 2)), dma((16,)), dma((32,)), dma((4, 2)),
            dma((BLOCKS + 4,)), dma((2,)), dma((2, 4)), dma((8,)), dma((BLOCKS,)), dma((2,)),
            dma((3, 2, NC)), dma((3, 2, NC)), dma((BLOCKS,)), dma((BLOCKS,)),
        ],
        compiler_params=pltpu.CompilerParams(
            collective_id=0, has_side_effects=True, vmem_limit_bytes=60 * MIB
        ),
        cost_estimate=pl.CostEstimate(
            flops=4 * QROWS * HD * CT * 24, bytes_accessed=20 * MIB, transcendentals=QROWS * CT * 24
        ),
        name="stretch_attention",
    )(queries, keys_values, mask, level, own, latents, gate_table)


def on_device(queries, keys_values, out_weight, latents, gate_table, noise_level, stretch_mask):
    return fused(queries, keys_values, stretch_mask, noise_level, out_weight, latents, gate_table)


def solution(mesh):
    rows = P(("stretch", "seq"), None)
    heads = P(("stretch", "seq"), None, None)
    return jax.shard_map(
        on_device,
        mesh=mesh,
        in_specs=(heads, heads, P("seq", None), rows, P(), P(), P()),
        out_specs=rows,
        check_vma=False,
    )
```

```python
import math

import jax
import jax.numpy as jnp
from jax import lax
from jax.experimental import pallas as pl
from jax.experimental.pallas import tpu as pltpu
from jax.sharding import PartitionSpec as P

MESH = pl.DeviceIdType.MESH
BIG = 1e30
MIB = 2**20
F32, BF16 = jnp.float32, jnp.bfloat16

ROWS = 48
CT = 384
HD = 128
GROUP = 3
SEQ = 8
QROWS = CT * GROUP
D = 6144
EXP_SCALE = math.log2(math.e) / math.sqrt(HD)

NC = 8
BLOCKS = 16


def kernel(
    q_hbm, kv_hbm, mask_hbm, level_hbm, own_hbm, lat_hbm, gate_hbm, out_ref,
    q_raw, kv_raw, q_ref, kv_ref, mask_ref, level_ref, q_far, att_far, mate_att, blend, lse, lse_partner, lse_mate, kvr, qr, qt, slots, acc, run_max, run_sum, att, att_in, rows_in,
    own_w, other_w, part, sends, recvs, lat, gate, done,
    mate_send, mate_recv, kv_send, kv_recv, q_send, q_recv, z_send, down_send, x_send, relay_send, sib_send, slot_recv, half_recv,
    load_sem, w_edge_send, w_send, w_sib_send, w_recv, swap_sem, ring_send, ring_recv, out_send, out_recv,
):
    c = lax.axis_index("stretch")
    s = lax.axis_index("seq")
    z, x, k = c // 8, (c // 2) % 4, c % 2
    zh, y = s // 4, s % 4
    bottom = 1 - (z + 3) // 4
    planes = 2 + z // 2 - z // 3

    def dev(zz, xx, kk):
        return ((zz * 4 + xx) * 2 + kk, s)

    def z_next(step):
        pos = (zh * 4 + z + step + 8) % 8
        return (((pos % 4) * 4 + x) * 2 + k, (pos // 4) * 4 + y)

    sibling = dev(z, x, 1 - k)
    above = z_next(1)
    outward = 2 * (z // 3) - 1
    mate = dev(3 - z, x, k)
    x_right, x_left = dev(z, (x + 1) % 4, k), dev(z, (x + 3) % 4, k)
    partner = (c, (s + 4) % SEQ)
    y_up, y_down = (c, zh * 4 + (y + 1) % 4), (c, zh * 4 + (y + 3) % 4)
    after, before = ((c + 1) % 32, s), ((c + 31) % 32, s)

    def push(src, dst, send, recv, target):
        return pltpu.make_async_remote_copy(
            src_ref=src, dst_ref=dst, send_sem=send, recv_sem=recv, device_id=target, device_id_type=MESH
        )

    def load_own(b):
        return pltpu.make_async_copy(own_hbm.at[:, pl.ds(b * CT, CT)], own_w.at[b], load_sem.at[b])

    load_lat = pltpu.make_async_copy(lat_hbm, lat, load_sem.at[BLOCKS])
    load_gate = pltpu.make_async_copy(gate_hbm, gate, load_sem.at[BLOCKS + 1])
    load_mask = pltpu.make_async_copy(mask_hbm, mask_ref, load_sem.at[BLOCKS + 2])
    load_level = pltpu.make_async_copy(level_hbm, level_ref, load_sem.at[BLOCKS + 3])

    barrier = pltpu.get_barrier_semaphore()
    greeted = [(c, (s + d) % SEQ) for d in range(1, SEQ)] + [
        z_next(1), z_next(-1), x_right, x_left, sibling, mate, after, before,
    ]
    for target in greeted:
        pl.semaphore_signal(barrier, inc=1, device_id=target, device_id_type=MESH)
    load_kv = pltpu.make_async_copy(kv_hbm, kv_raw, load_sem.at[BLOCKS + 4])
    load_q = pltpu.make_async_copy(q_hbm, q_raw, load_sem.at[BLOCKS + 5])
    load_kv.start()
    load_q.start()
    load_mask.start()
    load_level.start()
    for b in range(BLOCKS):
        load_own(b).start()
    load_lat.start()
    load_gate.start()
    load_kv.wait()
    kv_ref[...] = jnp.transpose(kv_raw[...], (1, 0, 2))
    load_q.wait()
    q_ref[...] = jnp.transpose(q_raw[...], (1, 0, 2)).reshape(SEQ, GROUP, ROWS, HD)
    run_max[...] = jnp.full_like(run_max, -BIG)
    run_sum[...] = jnp.zeros_like(run_sum)
    acc[...] = jnp.zeros_like(acc)
    kvr[s] = kv_ref[s]
    qr[s] = q_ref[s]
    pl.semaphore_wait(barrier, len(greeted))

    def kv_copy(d):
        other = (s + d) % SEQ
        return push(kv_ref.at[other], kvr.at[s], kv_send.at[d], kv_recv.at[s], (c, other))

    def q_copy(d):
        other = (s + d) % SEQ
        return push(q_ref.at[other], qr.at[s], q_send.at[d], q_recv.at[s], (c, other))

    def landed(ref, recv, index):
        push(ref.at[index], ref.at[index], kv_send.at[0], recv.at[index], partner).wait_recv()

    for d in (4, 3, 5, 2, 6, 1, 7):
        kv_copy(d).start()
    def block_of(place):
        group = place // 4
        step = group + group // 2 - 2 * (group // 3)
        return 4 * ((x + step) % 4) + place % 4

    def w_push(source, b, send, target):
        return push(source.at[b], other_w.at[b], send, w_recv.at[b], target)

    def core_block(b):
        return block_of(4 * (b // 2) + 2 * k + b % 2)

    def w_edge(b):
        q = core_block(b)
        return push(own_hbm.at[:, pl.ds(pl.multiple_of(q * CT, CT), CT)], other_w.at[q], w_edge_send.at[b], w_recv.at[q], z_next(outward))

    def w_inward(b):
        return w_push(other_w, core_block(b), w_send.at[b, 0], z_next(-outward))

    def w_beside(b, way):
        target = (x_right, x_left)[way]
        return w_push(other_w, core_block(b), w_send.at[b, 1 + way], target)

    def w_across(half):
        moved = core_block(2 * (2 - half) + half)
        return w_push(other_w, moved, w_send.at[half, 3], x_left if half else x_right)

    def w_sib(b):
        return w_push(other_w, core_block(b), w_sib_send.at[b], sibling)

    def w_wait(b):
        w_push(other_w, b, w_sib_send.at[0], sibling).wait_recv()

    def w_spread(b):
        w_wait(core_block(b))

        @pl.when(z % 3 == 0)
        def _():
            w_inward(b).start()

        for way in range(2):
            w_beside(b, way).start()
        w_sib(b).start()

    def w_hand_over(b):
        w_wait(core_block(b))
        w_sib(b).start()

    @pl.when(z % 3 == 0)
    def _():
        for b in range(2):
            w_edge(b).start()

    for d in (4, 3, 5, 2, 6, 1, 7):
        kv_copy(d).wait_send()
    for d in (4, 3, 5, 2, 6, 1, 7):
        q_copy(d).start()
    for d in range(1, SEQ):
        landed(kvr, kv_recv, (s + d) % SEQ)
    block = kvr[...].reshape(CT, 2 * HD)
    slots[c, 0:CT, :] = block[:, :HD]
    value_t = jnp.transpose(block[:, HD:].astype(F32)).astype(BF16)
    for t in range(3):
        slots[c, CT + t * HD : CT + (t + 1) * HD, :] = value_t[:, t * HD : (t + 1) * HD]

    def slot_push(j, send, target):
        return push(slots.at[j], slots.at[j], send, slot_recv.at[j], target)

    def plane_of(t):
        return z - t + 2 * t * bottom

    def column_slot(t):
        return (plane_of(t) * 4 + x) * 2 + k

    def z_copy(t):
        return slot_push(column_slot(t), z_send.at[t], above)

    def x_copy(t, right):
        return slot_push(column_slot(t), x_send.at[t, right], x_right if right else x_left)

    def pair_of(n):
        t, i = n // 4, n % 4
        step = i + i // 2 - 2 * (i // 3)
        return plane_of(t) * 4 + (x + step) % 4

    def sib_copy(n):
        return slot_push(2 * pair_of(n) + k, sib_send.at[n], sibling)

    def half_of(t, pair, right):
        part_of = slots.at[2 * pair + k, pl.ds(CT * right, CT)]
        return push(
            part_of, part_of, relay_send.at[t, right], half_recv.at[t, right], x_right if right else x_left
        )

    def relay(t, right):
        return half_of(t, plane_of(t) * 4 + (x + 1 + 2 * right) % 4, right)

    def wait_slot(j):
        slot_push(j, z_send.at[0], sibling).wait_recv()

    def down_copy():
        return slot_push(column_slot(0), down_send.at[0], z_next(-1))

    def spread(t):
        @pl.when((z == 1) | ((z % 2 == 0) & (t == 0)))
        def _():
            z_copy(t).start()

        @pl.when((z == 1) & (t == 0))
        def _():
            down_copy().start()

        x_copy(t, 0).start()
        x_copy(t, 1).start()
        sib_copy(4 * t).start()

    def from_beside(t, right):
        n = 4 * t + 1 + right
        wait_slot(2 * pair_of(n) + k)
        relay(t, right).start()
        sib_copy(n).start()

    def from_across(t):
        n = 4 * t + 3
        for right in range(2):
            half_of(t, pair_of(n), right).wait_recv()
        sib_copy(n).start()

    def pass_on(t):
        wait_slot(column_slot(t))
        spread(t)

    spread(0)
    from_beside(0, 0)
    from_beside(0, 1)

    pass_on(1)

    for d in range(1, SEQ):
        landed(qr, q_recv, (s + d) % SEQ)
    q_mate = push(qr, q_far, mate_send.at[0], mate_recv.at[0], mate)

    @pl.when(z == 3)
    def _():
        q_mate.start()

    def take_queries(source):
        qt[...] = jnp.transpose(source[...].reshape(QROWS, HD).astype(F32)).astype(BF16)

    take_queries(qr)
    for b in range(BLOCKS):
        load_own(b).wait()


    load_mask.wait()
    load_level.wait()

    own_pair = z * 4 + x
    swap = push(att.at[pl.ds(4 * (1 - zh), 4)], att_in, swap_sem.at[0], swap_sem.at[1], partner)
    lse_swap = push(lse, lse_partner, mate_send.at[1], mate_recv.at[1], partner)

    def mate_part(near, target):
        half = zh if near else 1 - zh
        at = 0 if near else 1
        return (
            push(att_far.at[pl.ds(4 * half, 4)], mate_att.at[at], mate_send.at[2 + at], mate_recv.at[2 + at], target),
            push(lse, lse_mate.at[at], mate_send.at[4 + at], mate_recv.at[4 + at], target),
        )

    def finish(target):
        total_weight = jnp.maximum(run_sum[...], 1e-30)
        out = jnp.transpose(acc[...] * (1.0 / total_weight)).astype(BF16)
        target[...] = out.reshape(SEQ, GROUP, ROWS, HD)
        lse[...] = jnp.broadcast_to(run_max[...] * EXP_SCALE + jnp.log2(total_weight), lse.shape)

    def attend(pair, row):
        ja = 2 * pair
        hide_a = jnp.where(mask_ref[row, ja] == 1, 0.0, 2 * BIG).astype(F32)
        hide_b = jnp.where(mask_ref[row, ja + 1] == 1, 0.0, 2 * BIG).astype(F32)
        ones = jnp.ones((16, CT), BF16)

        def values(j):
            cut = [slots[j, CT + t * HD : CT + (t + 1) * HD, :] for t in range(3)]
            return jnp.concatenate([jnp.concatenate(cut, axis=1), ones], axis=0)

        va, vb = values(ja), values(ja + 1)
        ka, kb = slots[ja, 0:CT, :], slots[ja + 1, 0:CT, :]

        def score(r):
            q_cols = qt[:, r * CT : (r + 1) * CT]
            return (
                jnp.dot(ka, q_cols, preferred_element_type=F32),
                jnp.dot(kb, q_cols, preferred_element_type=F32),
            )

        scores = [score(r) for r in range(GROUP)]
        for r in range(GROUP):
            sa, sb = scores[r]
            cols = slice(r * CT, (r + 1) * CT)
            top = jnp.maximum(
                jnp.max(sa, axis=0, keepdims=True) - hide_a, jnp.max(sb, axis=0, keepdims=True) - hide_b
            )
            old = run_max[:, cols]
            new = jnp.maximum(old, top)
            factor = jnp.exp2((old - new) * EXP_SCALE)
            pa = jnp.exp2((sa - (new + hide_a)) * EXP_SCALE)
            pb = jnp.exp2((sb - (new + hide_b)) * EXP_SCALE)
            run_max[:, cols] = new
            update = jnp.dot(va, pa.astype(BF16), preferred_element_type=F32) + jnp.dot(
                vb, pb.astype(BF16), preferred_element_type=F32
            )
            run_sum[:, cols] = run_sum[:, cols] * factor + update[HD : HD + 1]
            acc[:, cols] = acc[:, cols] * factor + update[:HD]

    w_first = jnp.where(z == 0, 1, jnp.where(z == 1, 4, jnp.where(z == 2, 8, 1)))
    w_count = 2

    def step(n, carry):
        t, i = (n // 4) // (1 + bottom), n % 4
        fresh = (bottom == 0) | (n // 4 != 1)
        for_mate = (bottom == 1) & (n >= 4)
        pair = pair_of(4 * t + i)

        @pl.when((bottom == 1) & (n == 4))
        def _():
            finish(att)
            swap.start()
            q_mate.wait_recv()
            take_queries(q_far)
            run_max[...] = jnp.full_like(run_max, -BIG)
            run_sum[...] = jnp.zeros_like(run_sum)
            acc[...] = jnp.zeros_like(acc)

        @pl.when(fresh)
        def _():
            wait_slot(2 * pair + 1 - k)

        @pl.when((pair <= own_pair) | for_mate)
        def _():
            attend(pair, c + 24 * bottom * ((n + 8) // 12))

        @pl.when((n == 1) & (z == 2))
        def _():
            pass_on(2)

        @pl.when((i == 1) & fresh)
        def _():
            from_across(t)

        @pl.when((i == 3) & (n // 4 + 1 < planes))
        def _():
            from_beside(n // 4 + 1, 0)
            from_beside(n // 4 + 1, 1)

        turn = n - w_first

        @pl.when((turn >= 0) & (turn % 2 == 0) & (turn < 2 * w_count))
        def _():
            w_spread(turn // 2)

        return carry

    lax.fori_loop(0, 4 * (planes + bottom), step, 0)

    @pl.when(z == 0)
    def _():
        finish(att_far)
        for copy in mate_part(True, mate) + mate_part(False, z_next(-1)):
            copy.start()

    @pl.when(z != 0)
    def _():
        finish(att)
        swap.start()

    @pl.when(z == 3)
    def _():
        lse_swap.start()

    def gather_rows(source, first, place):
        for h in range(GROUP):
            rows_in[place, :, h * HD : (h + 1) * HD] = source[pl.ds(first, 4), h].reshape(4 * ROWS, HD)

    def blended(near, lse_home, lse_far, home, far):
        top = jnp.maximum(lse_home, lse_far)
        home_weight, far_weight = jnp.exp2(lse_home - top), jnp.exp2(lse_far - top)
        share = jnp.broadcast_to(home_weight / (home_weight + far_weight), (HD, QROWS))
        blend[...] = jnp.transpose(share).reshape(SEQ, GROUP, ROWS, HD)
        part_of = blend[pl.ds(4 * zh, 4)]
        mixed = part_of * home.astype(F32) + (1.0 - part_of) * far.astype(F32)
        return mixed.astype(BF16)

    for group in (1, 2):
        for half in range(2):
            w_hand_over(2 * group + half)
        w_across(2 - group).start()
    swap.wait()

    @pl.when(z == 3)
    def _():
        lse_swap.wait()
        for copy in mate_part(True, mate) + mate_part(False, mate):
            copy.wait_recv()
        att[pl.ds(4 * zh, 4)] = blended(True, lse[0:1], lse_mate[0, 0:1], att[pl.ds(4 * zh, 4)], mate_att[0])
        att_in[...] = blended(False, lse_partner[0:1], lse_mate[1, 0:1], att_in[...], mate_att[1])

    gather_rows(att, 4 * zh, 0)
    gather_rows(att_in, 0, 1)

    def ring(hop, dirn, j):
        target = y_up if (dirn == 0) == (hop < 2) else y_down
        return push(
            sends.at[hop, dirn, j], recvs.at[hop, dirn, j],
            ring_send.at[hop, dirn, j], ring_recv.at[hop, dirn, j], target,
        )

    def columns(place):
        return pl.ds(pl.multiple_of(block_of(place) * CT, CT), CT)

    def final(place):
        cols = columns(place)
        return push(done.at[:, cols], out_ref.at[:, cols], out_send.at[place], out_recv.at[place], after)

    load_lat.wait()
    load_gate.wait()
    level = level_ref[c]

    def first(j):
        @pl.when(j % 2 != k)
        def _():
            for dirn in range(2):
                w_wait(block_of(2 * j + dirn))

        for dirn in range(2):
            q = block_of(2 * j + dirn)
            product = jnp.dot(rows_in[0], own_w[q], preferred_element_type=F32)
            product += jnp.dot(rows_in[1], other_w[q], preferred_element_type=F32)
            part[dirn, j] = product.reshape(4, ROWS, CT)
            sends[0, dirn, j] = part[dirn, j, (y + 2) % 4].astype(BF16)
            ring(0, dirn, j).start()
        for dirn in range(2):
            sends[2, dirn, j] = part[dirn, j, (y + 3 - 2 * dirn) % 4].astype(BF16)
            ring(2, dirn, j).start()

    def middle(j):
        for dirn in range(2):
            ring(0, dirn, j).wait_recv()
            sends[1, dirn, j] = (
                recvs[0, dirn, j].astype(F32) + part[dirn, j, (y + 1 + 2 * dirn) % 4]
            ).astype(BF16)
            ring(1, dirn, j).start()

    def last(j):
        for dirn in range(2):
            cols = columns(2 * j + dirn)
            ring(1, dirn, j).wait_recv()
            ring(2, dirn, j).wait_recv()
            branch = recvs[1, dirn, j].astype(F32) + recvs[2, dirn, j].astype(F32) + part[dirn, j, y]
            gate_row = gate[pl.ds(level, 1), cols]
            done[:, cols] = (lat[:, cols].astype(F32) + gate_row * branch).astype(BF16)
            final(2 * j + dirn).start()

    def run(lo, hi, work):
        def body(j, carry):
            work(j)
            return carry

        lax.fori_loop(lo, hi, body, 0)

    run(0, 4, first)
    run(0, 4, middle)
    run(4, 6, first)
    w_hand_over(6)
    w_hand_over(7)
    run(6, 8, first)
    run(4, 6, middle)
    run(0, 4, last)
    run(6, 8, middle)
    run(4, 8, last)

    for d in range(1, SEQ):
        q_copy(d).wait_send()

    def drain_plane(t, carry):
        @pl.when((z == 1) | ((z % 2 == 0) & (t == 0)))
        def _():
            z_copy(t).wait_send()

        for right in range(2):
            x_copy(t, right).wait_send()
            relay(t, right).wait_send()
        return carry

    @pl.when(z == 1)
    def _():
        down_copy().wait_send()

    @pl.when(z == 0)
    def _():
        for copy in mate_part(True, mate) + mate_part(False, z_next(-1)):
            copy.wait_send()

    @pl.when(z == 3)
    def _():
        q_mate.wait_send()

    def drain_sib(n, carry):
        sib_copy(n).wait_send()
        return carry

    for b in range(2):
        @pl.when(z % 3 == 0)
        def _(b=b):
            w_edge(b).wait_send()
            w_inward(b).wait_send()

        for way in range(2):
            w_beside(b, way).wait_send()
        w_across(b).wait_send()
    for b in range(8):
        w_sib(b).wait_send()

    def drain_ring(j, carry):
        for dirn in range(2):
            for hop in range(3):
                ring(hop, dirn, j).wait_send()
            final(2 * j + dirn).wait()
        return carry

    lax.fori_loop(0, planes, drain_plane, 0)
    lax.fori_loop(0, 4 * planes, drain_sib, 0)
    lax.fori_loop(0, NC, drain_ring, 0)


def fused(queries, keys_values, mask, level, own, latents, gate_table):
    anywhere = pl.BlockSpec(memory_space=pl.ANY)
    dma = pltpu.SemaphoreType.DMA
    return pl.pallas_call(
        kernel,
        out_shape=jax.ShapeDtypeStruct((ROWS, D), BF16),
        in_specs=[anywhere] * 7,
        out_specs=anywhere,
        scratch_shapes=[
            pltpu.VMEM((ROWS, SEQ * GROUP, HD), BF16),
            pltpu.VMEM((ROWS, SEQ, 2 * HD), BF16),
            pltpu.VMEM((SEQ, GROUP, ROWS, HD), BF16),
            pltpu.VMEM((SEQ, ROWS, 2 * HD), BF16),
            pltpu.SMEM((32, 32), jnp.int32),
            pltpu.SMEM((32,), jnp.int32),
            pltpu.VMEM((SEQ, GROUP, ROWS, HD), BF16),
            pltpu.VMEM((SEQ, GROUP, ROWS, HD), BF16),
            pltpu.VMEM((2, 4, GROUP, ROWS, HD), BF16),
            pltpu.VMEM((SEQ, GROUP, ROWS, HD), F32),
            pltpu.VMEM((8, QROWS), F32),
            pltpu.VMEM((8, QROWS), F32),
            pltpu.VMEM((2, 8, QROWS), F32),
            pltpu.VMEM((SEQ, ROWS, 2 * HD), BF16),
            pltpu.VMEM((SEQ, GROUP, ROWS, HD), BF16),
            pltpu.VMEM((HD, QROWS), BF16),
            pltpu.VMEM((32, 2 * CT, HD), BF16),
            pltpu.VMEM((HD, QROWS), F32),
            pltpu.VMEM((1, QROWS), F32),
            pltpu.VMEM((1, QROWS), F32),
            pltpu.VMEM((SEQ, GROUP, ROWS, HD), BF16),
            pltpu.VMEM((4, GROUP, ROWS, HD), BF16),
            pltpu.VMEM((2, 4 * ROWS, CT), BF16),
            pltpu.VMEM((BLOCKS, CT, CT), BF16),
            pltpu.VMEM((BLOCKS, CT, CT), BF16),
            pltpu.VMEM((2, NC, 4, ROWS, CT), F32),
            pltpu.VMEM((3, 2, NC, ROWS, CT), BF16),
            pltpu.VMEM((3, 2, NC, ROWS, CT), BF16),
            pltpu.VMEM((ROWS, D), BF16),
            pltpu.VMEM((64, D), F32),
            pltpu.VMEM((ROWS, D), BF16),
            dma((6,)), dma((6,)), dma((SEQ,)), dma((SEQ,)), dma((SEQ,)), dma((SEQ,)),
            dma((4,)), dma((1,)), dma((4, 2)), dma((4, 2)), dma((16,)), dma((32,)), dma((4, 2)),
            dma((BLOCKS + 6,)), dma((2,)), dma((2, 4)), dma((8,)), dma((BLOCKS,)), dma((2,)),
            dma((3, 2, NC)), dma((3, 2, NC)), dma((BLOCKS,)), dma((BLOCKS,)),
        ],
        compiler_params=pltpu.CompilerParams(
            collective_id=0, has_side_effects=True, vmem_limit_bytes=60 * MIB
        ),
        cost_estimate=pl.CostEstimate(
            flops=4 * QROWS * HD * CT * 24, bytes_accessed=20 * MIB, transcendentals=QROWS * CT * 24
        ),
        name="stretch_attention",
    )(queries, keys_values, mask, level, own, latents, gate_table)


def on_device(queries, keys_values, out_weight, latents, gate_table, noise_level, stretch_mask):
    return fused(queries, keys_values, stretch_mask, noise_level, out_weight, latents, gate_table)


def solution(mesh):
    rows = P(("stretch", "seq"), None)
    heads = P(("stretch", "seq"), None, None)
    return jax.shard_map(
        on_device,
        mesh=mesh,
        in_specs=(heads, heads, P("seq", None), rows, P(), P(), P()),
        out_specs=rows,
        check_vma=False,
    )
```

```python
import math

import jax
import jax.numpy as jnp
from jax import lax
from jax.experimental import pallas as pl
from jax.experimental.pallas import tpu as pltpu
from jax.sharding import PartitionSpec as P

MESH = pl.DeviceIdType.MESH
BIG = 1e30
MIB = 2**20
F32, BF16 = jnp.float32, jnp.bfloat16

ROWS = 48
CT = 384
HD = 128
GROUP = 3
SEQ = 8
QROWS = CT * GROUP
D = 6144
EXP_SCALE = math.log2(math.e) / math.sqrt(HD)

NC = 8
BLOCKS = 16


def kernel(
    q_hbm, kv_hbm, mask_hbm, level_hbm, own_hbm, lat_hbm, gate_hbm, out_ref,
    q_raw, kv_raw, q_ref, kv_ref, mask_ref, level_ref, q_far, att_far, mate_att, blend, lse, lse_partner, lse_mate, kvr, qr, qt, slots, acc, run_max, run_sum, att, att_in, rows_in,
    own_w, other_w, part, sends, recvs, lat, gate, done,
    mate_send, mate_recv, kv_send, kv_recv, q_send, q_recv, z_send, down_send, x_send, relay_send, sib_send, slot_recv, half_recv,
    load_sem, w_edge_send, w_send, w_sib_send, w_recv, swap_sem, ring_send, ring_recv, out_send, out_recv,
):
    c = lax.axis_index("stretch")
    s = lax.axis_index("seq")
    z, x, k = c // 8, (c // 2) % 4, c % 2
    zh, y = s // 4, s % 4
    bottom = 1 - (z + 3) // 4
    planes = 2 + z // 2 - z // 3

    def dev(zz, xx, kk):
        return ((zz * 4 + xx) * 2 + kk, s)

    def z_next(step):
        pos = (zh * 4 + z + step + 8) % 8
        return (((pos % 4) * 4 + x) * 2 + k, (pos // 4) * 4 + y)

    sibling = dev(z, x, 1 - k)
    above = z_next(1)
    outward = 2 * (z // 3) - 1
    mate = dev(3 - z, x, k)
    x_right, x_left = dev(z, (x + 1) % 4, k), dev(z, (x + 3) % 4, k)
    partner = (c, (s + 4) % SEQ)
    y_up, y_down = (c, zh * 4 + (y + 1) % 4), (c, zh * 4 + (y + 3) % 4)
    after, before = ((c + 1) % 32, s), ((c + 31) % 32, s)

    def push(src, dst, send, recv, target):
        return pltpu.make_async_remote_copy(
            src_ref=src, dst_ref=dst, send_sem=send, recv_sem=recv, device_id=target, device_id_type=MESH
        )

    def load_own(b):
        return pltpu.make_async_copy(own_hbm.at[:, pl.ds(b * CT, CT)], own_w.at[b], load_sem.at[b])

    load_lat = pltpu.make_async_copy(lat_hbm, lat, load_sem.at[BLOCKS])
    load_gate = pltpu.make_async_copy(gate_hbm, gate, load_sem.at[BLOCKS + 1])
    load_mask = pltpu.make_async_copy(mask_hbm, mask_ref, load_sem.at[BLOCKS + 2])
    load_level = pltpu.make_async_copy(level_hbm, level_ref, load_sem.at[BLOCKS + 3])

    barrier = pltpu.get_barrier_semaphore()
    greeted = [(c, (s + d) % SEQ) for d in range(1, SEQ)] + [
        z_next(1), z_next(-1), x_right, x_left, sibling, mate, after, before,
    ]
    for target in greeted:
        pl.semaphore_signal(barrier, inc=1, device_id=target, device_id_type=MESH)
    load_kv = pltpu.make_async_copy(kv_hbm, kv_raw, load_sem.at[BLOCKS + 4])
    load_q = pltpu.make_async_copy(q_hbm, q_raw, load_sem.at[BLOCKS + 5])
    load_kv.start()
    load_q.start()
    load_mask.start()
    load_level.start()
    for b in range(BLOCKS):
        load_own(b).start()
    load_lat.start()
    load_gate.start()
    load_kv.wait()
    kv_ref[...] = jnp.transpose(kv_raw[...], (1, 0, 2))
    load_q.wait()
    q_ref[...] = jnp.transpose(q_raw[...], (1, 0, 2)).reshape(SEQ, GROUP, ROWS, HD)
    run_max[...] = jnp.full_like(run_max, -BIG)
    run_sum[...] = jnp.zeros_like(run_sum)
    acc[...] = jnp.zeros_like(acc)
    kvr[s] = kv_ref[s]
    qr[s] = q_ref[s]
    pl.semaphore_wait(barrier, len(greeted))

    def kv_copy(d):
        other = (s + d) % SEQ
        return push(kv_ref.at[other], kvr.at[s], kv_send.at[d], kv_recv.at[s], (c, other))

    def q_copy(d):
        other = (s + d) % SEQ
        return push(q_ref.at[other], qr.at[s], q_send.at[d], q_recv.at[s], (c, other))

    def landed(ref, recv, index):
        push(ref.at[index], ref.at[index], kv_send.at[0], recv.at[index], partner).wait_recv()

    for d in (4, 3, 5, 2, 6, 1, 7):
        kv_copy(d).start()
    def block_of(place):
        group = place // 4
        step = group + group // 2 - 2 * (group // 3)
        return 4 * ((x + step) % 4) + place % 4

    def w_push(source, b, send, target):
        return push(source.at[b], other_w.at[b], send, w_recv.at[b], target)

    def core_block(b):
        return block_of(4 * (b // 2) + 2 * k + b % 2)

    def w_edge(b):
        q = core_block(b)
        return push(own_hbm.at[:, pl.ds(pl.multiple_of(q * CT, CT), CT)], other_w.at[q], w_edge_send.at[b], w_recv.at[q], z_next(outward))

    def w_inward(b):
        return w_push(other_w, core_block(b), w_send.at[b, 0], z_next(-outward))

    def w_beside(b, way):
        target = (x_right, x_left)[way]
        return w_push(other_w, core_block(b), w_send.at[b, 1 + way], target)

    def w_across(half):
        moved = core_block(2 * (2 - half) + half)
        return w_push(other_w, moved, w_send.at[half, 3], x_left if half else x_right)

    def w_sib(b):
        return w_push(other_w, core_block(b), w_sib_send.at[b], sibling)

    def w_wait(b):
        w_push(other_w, b, w_sib_send.at[0], sibling).wait_recv()

    def w_spread(b):
        w_wait(core_block(b))

        @pl.when(z % 3 == 0)
        def _():
            w_inward(b).start()

        for way in range(2):
            w_beside(b, way).start()
        w_sib(b).start()

    def w_hand_over(b):
        w_wait(core_block(b))
        w_sib(b).start()

    @pl.when(z % 3 == 0)
    def _():
        for b in range(2):
            w_edge(b).start()

    for d in (4, 3, 5, 2, 6, 1, 7):
        kv_copy(d).wait_send()
    for d in (4, 3, 5, 2, 6, 1, 7):
        q_copy(d).start()
    for d in range(1, SEQ):
        landed(kvr, kv_recv, (s + d) % SEQ)
    block = kvr[...].reshape(CT, 2 * HD)
    slots[c, 0:CT, :] = block[:, :HD]
    value_t = jnp.transpose(block[:, HD:].astype(F32)).astype(BF16)
    for t in range(3):
        slots[c, CT + t * HD : CT + (t + 1) * HD, :] = value_t[:, t * HD : (t + 1) * HD]

    def slot_push(j, send, target):
        return push(slots.at[j], slots.at[j], send, slot_recv.at[j], target)

    def plane_of(t):
        return z - t + 2 * t * bottom

    def column_slot(t):
        return (plane_of(t) * 4 + x) * 2 + k

    def z_copy(t):
        return slot_push(column_slot(t), z_send.at[t], above)

    def x_copy(t, right):
        return slot_push(column_slot(t), x_send.at[t, right], x_right if right else x_left)

    def pair_of(n):
        t, i = n // 4, n % 4
        step = i + i // 2 - 2 * (i // 3)
        return plane_of(t) * 4 + (x + step) % 4

    def sib_copy(n):
        return slot_push(2 * pair_of(n) + k, sib_send.at[n], sibling)

    def half_of(t, pair, right):
        part_of = slots.at[2 * pair + k, pl.ds(CT * right, CT)]
        return push(
            part_of, part_of, relay_send.at[t, right], half_recv.at[t, right], x_right if right else x_left
        )

    def relay(t, right):
        return half_of(t, plane_of(t) * 4 + (x + 1 + 2 * right) % 4, right)

    def wait_slot(j):
        slot_push(j, z_send.at[0], sibling).wait_recv()

    def down_copy():
        return slot_push(column_slot(0), down_send.at[0], z_next(-1))

    def spread(t):
        @pl.when((z == 1) | ((z % 2 == 0) & (t == 0)))
        def _():
            z_copy(t).start()

        @pl.when((z == 1) & (t == 0))
        def _():
            down_copy().start()

        x_copy(t, 0).start()
        x_copy(t, 1).start()
        sib_copy(4 * t).start()

    def from_beside(t, right):
        n = 4 * t + 1 + right
        wait_slot(2 * pair_of(n) + k)
        relay(t, right).start()
        sib_copy(n).start()

    def from_across(t):
        n = 4 * t + 3
        for right in range(2):
            half_of(t, pair_of(n), right).wait_recv()
        sib_copy(n).start()

    def pass_on(t):
        wait_slot(column_slot(t))
        spread(t)

    spread(0)
    from_beside(0, 0)
    from_beside(0, 1)

    pass_on(1)

    for d in range(1, SEQ):
        landed(qr, q_recv, (s + d) % SEQ)
    q_mate = push(qr, q_far, mate_send.at[0], mate_recv.at[0], mate)

    @pl.when(z == 3)
    def _():
        q_mate.start()

    def take_queries(source):
        qt[...] = jnp.transpose(source[...].reshape(QROWS, HD).astype(F32)).astype(BF16)

    take_queries(qr)
    for b in range(BLOCKS):
        load_own(b).wait()


    load_mask.wait()
    load_level.wait()

    own_pair = z * 4 + x
    swap = push(att.at[pl.ds(4 * (1 - zh), 4)], att_in, swap_sem.at[0], swap_sem.at[1], partner)
    lse_swap = push(lse, lse_partner, mate_send.at[1], mate_recv.at[1], partner)

    def mate_part(near, target):
        half = zh if near else 1 - zh
        at = 0 if near else 1
        return (
            push(att_far.at[pl.ds(4 * half, 4)], mate_att.at[at], mate_send.at[2 + at], mate_recv.at[2 + at], target),
            push(lse, lse_mate.at[at], mate_send.at[4 + at], mate_recv.at[4 + at], target),
        )

    def finish(target):
        total_weight = jnp.maximum(run_sum[...], 1e-30)
        out = jnp.transpose(acc[...] * (1.0 / total_weight)).astype(BF16)
        target[...] = out.reshape(SEQ, GROUP, ROWS, HD)
        lse[...] = jnp.broadcast_to(run_max[...] * EXP_SCALE + jnp.log2(total_weight), lse.shape)

    def attend(pair, row):
        ja = 2 * pair
        hide_a = jnp.where(mask_ref[row, ja] == 1, 0.0, 2 * BIG).astype(F32)
        hide_b = jnp.where(mask_ref[row, ja + 1] == 1, 0.0, 2 * BIG).astype(F32)
        ones = jnp.ones((16, CT), BF16)

        def values(j):
            cut = [slots[j, CT + t * HD : CT + (t + 1) * HD, :] for t in range(3)]
            return jnp.concatenate([jnp.concatenate(cut, axis=1), ones], axis=0)

        va, vb = values(ja), values(ja + 1)
        ka, kb = slots[ja, 0:CT, :], slots[ja + 1, 0:CT, :]

        def score(r):
            q_cols = qt[:, r * CT : (r + 1) * CT]
            return (
                jnp.dot(ka, q_cols, preferred_element_type=F32),
                jnp.dot(kb, q_cols, preferred_element_type=F32),
            )

        scores = [score(r) for r in range(GROUP)]
        for r in range(GROUP):
            sa, sb = scores[r]
            cols = slice(r * CT, (r + 1) * CT)
            top = jnp.maximum(
                jnp.max(sa, axis=0, keepdims=True) - hide_a, jnp.max(sb, axis=0, keepdims=True) - hide_b
            )
            old = run_max[:, cols]
            new = jnp.maximum(old, top)
            factor = jnp.exp2((old - new) * EXP_SCALE)
            pa = jnp.exp2((sa - (new + hide_a)) * EXP_SCALE)
            pb = jnp.exp2((sb - (new + hide_b)) * EXP_SCALE)
            run_max[:, cols] = new
            update = jnp.dot(va, pa.astype(BF16), preferred_element_type=F32) + jnp.dot(
                vb, pb.astype(BF16), preferred_element_type=F32
            )
            run_sum[:, cols] = run_sum[:, cols] * factor + update[HD : HD + 1]
            acc[:, cols] = acc[:, cols] * factor + update[:HD]

    w_first = jnp.where(z == 0, 1, jnp.where(z == 1, 5, jnp.where(z == 2, 8, 2)))
    w_count = 2

    def step(n, carry):
        t, i = (n // 4) // (1 + bottom), n % 4
        fresh = (bottom == 0) | (n // 4 != 1)
        for_mate = (bottom == 1) & (n >= 4)
        pair = pair_of(4 * t + i)

        @pl.when((bottom == 1) & (n == 4))
        def _():
            finish(att)
            swap.start()
            q_mate.wait_recv()
            take_queries(q_far)
            run_max[...] = jnp.full_like(run_max, -BIG)
            run_sum[...] = jnp.zeros_like(run_sum)
            acc[...] = jnp.zeros_like(acc)

        @pl.when(fresh)
        def _():
            wait_slot(2 * pair + 1 - k)

        @pl.when((pair <= own_pair) | for_mate)
        def _():
            attend(pair, c + 24 * bottom * ((n + 8) // 12))

        @pl.when((n == 1) & (z == 2))
        def _():
            pass_on(2)

        @pl.when((i == 1) & fresh)
        def _():
            from_across(t)

        @pl.when((i == 3) & (n // 4 + 1 < planes))
        def _():
            from_beside(n // 4 + 1, 0)
            from_beside(n // 4 + 1, 1)

        turn = n - w_first

        @pl.when((turn >= 0) & (turn % 2 == 0) & (turn < 2 * w_count))
        def _():
            w_spread(turn // 2)

        return carry

    lax.fori_loop(0, 4 * (planes + bottom), step, 0)

    @pl.when(z == 0)
    def _():
        finish(att_far)
        for copy in mate_part(True, mate) + mate_part(False, z_next(-1)):
            copy.start()

    @pl.when(z != 0)
    def _():
        finish(att)
        swap.start()

    @pl.when(z == 3)
    def _():
        lse_swap.start()

    def gather_rows(source, first, place):
        for h in range(GROUP):
            rows_in[place, :, h * HD : (h + 1) * HD] = source[pl.ds(first, 4), h].reshape(4 * ROWS, HD)

    def blended(near, lse_home, lse_far, home, far):
        top = jnp.maximum(lse_home, lse_far)
        home_weight, far_weight = jnp.exp2(lse_home - top), jnp.exp2(lse_far - top)
        share = jnp.broadcast_to(home_weight / (home_weight + far_weight), (HD, QROWS))
        blend[...] = jnp.transpose(share).reshape(SEQ, GROUP, ROWS, HD)
        part_of = blend[pl.ds(4 * zh, 4)]
        mixed = part_of * home.astype(F32) + (1.0 - part_of) * far.astype(F32)
        return mixed.astype(BF16)

    for group in (1, 2):
        for half in range(2):
            w_hand_over(2 * group + half)
        w_across(2 - group).start()
    swap.wait()

    @pl.when(z == 3)
    def _():
        lse_swap.wait()
        for copy in mate_part(True, mate) + mate_part(False, mate):
            copy.wait_recv()
        att[pl.ds(4 * zh, 4)] = blended(True, lse[0:1], lse_mate[0, 0:1], att[pl.ds(4 * zh, 4)], mate_att[0])
        att_in[...] = blended(False, lse_partner[0:1], lse_mate[1, 0:1], att_in[...], mate_att[1])

    gather_rows(att, 4 * zh, 0)
    gather_rows(att_in, 0, 1)

    def ring(hop, dirn, j):
        target = y_up if (dirn == 0) == (hop < 2) else y_down
        return push(
            sends.at[hop, dirn, j], recvs.at[hop, dirn, j],
            ring_send.at[hop, dirn, j], ring_recv.at[hop, dirn, j], target,
        )

    def columns(place):
        return pl.ds(pl.multiple_of(block_of(place) * CT, CT), CT)

    def final(place):
        cols = columns(place)
        return push(done.at[:, cols], out_ref.at[:, cols], out_send.at[place], out_recv.at[place], after)

    load_lat.wait()
    load_gate.wait()
    level = level_ref[c]

    def first(j):
        @pl.when(j % 2 != k)
        def _():
            for dirn in range(2):
                w_wait(block_of(2 * j + dirn))

        for dirn in range(2):
            q = block_of(2 * j + dirn)
            product = jnp.dot(rows_in[0], own_w[q], preferred_element_type=F32)
            product += jnp.dot(rows_in[1], other_w[q], preferred_element_type=F32)
            part[dirn, j] = product.reshape(4, ROWS, CT)
            sends[0, dirn, j] = part[dirn, j, (y + 2) % 4].astype(BF16)
            ring(0, dirn, j).start()
        for dirn in range(2):
            sends[2, dirn, j] = part[dirn, j, (y + 3 - 2 * dirn) % 4].astype(BF16)
            ring(2, dirn, j).start()

    def middle(j):
        for dirn in range(2):
            ring(0, dirn, j).wait_recv()
            sends[1, dirn, j] = (
                recvs[0, dirn, j].astype(F32) + part[dirn, j, (y + 1 + 2 * dirn) % 4]
            ).astype(BF16)
            ring(1, dirn, j).start()

    def last(j):
        for dirn in range(2):
            cols = columns(2 * j + dirn)
            ring(1, dirn, j).wait_recv()
            ring(2, dirn, j).wait_recv()
            branch = recvs[1, dirn, j].astype(F32) + recvs[2, dirn, j].astype(F32) + part[dirn, j, y]
            gate_row = gate[pl.ds(level, 1), cols]
            done[:, cols] = (lat[:, cols].astype(F32) + gate_row * branch).astype(BF16)
            final(2 * j + dirn).start()

    def run(lo, hi, work):
        def body(j, carry):
            work(j)
            return carry

        lax.fori_loop(lo, hi, body, 0)

    run(0, 4, first)
    run(0, 4, middle)
    w_hand_over(6)
    w_hand_over(7)
    run(4, 8, first)
    run(0, 4, last)
    run(4, 8, middle)
    run(4, 8, last)

    for d in range(1, SEQ):
        q_copy(d).wait_send()

    def drain_plane(t, carry):
        @pl.when((z == 1) | ((z % 2 == 0) & (t == 0)))
        def _():
            z_copy(t).wait_send()

        for right in range(2):
            x_copy(t, right).wait_send()
            relay(t, right).wait_send()
        return carry

    @pl.when(z == 1)
    def _():
        down_copy().wait_send()

    @pl.when(z == 0)
    def _():
        for copy in mate_part(True, mate) + mate_part(False, z_next(-1)):
            copy.wait_send()

    @pl.when(z == 3)
    def _():
        q_mate.wait_send()

    def drain_sib(n, carry):
        sib_copy(n).wait_send()
        return carry

    for b in range(2):
        @pl.when(z % 3 == 0)
        def _(b=b):
            w_edge(b).wait_send()
            w_inward(b).wait_send()

        for way in range(2):
            w_beside(b, way).wait_send()
        w_across(b).wait_send()
    for b in range(8):
        w_sib(b).wait_send()

    def drain_ring(j, carry):
        for dirn in range(2):
            for hop in range(3):
                ring(hop, dirn, j).wait_send()
            final(2 * j + dirn).wait()
        return carry

    lax.fori_loop(0, planes, drain_plane, 0)
    lax.fori_loop(0, 4 * planes, drain_sib, 0)
    lax.fori_loop(0, NC, drain_ring, 0)


def fused(queries, keys_values, mask, level, own, latents, gate_table):
    anywhere = pl.BlockSpec(memory_space=pl.ANY)
    dma = pltpu.SemaphoreType.DMA
    return pl.pallas_call(
        kernel,
        out_shape=jax.ShapeDtypeStruct((ROWS, D), BF16),
        in_specs=[anywhere] * 7,
        out_specs=anywhere,
        scratch_shapes=[
            pltpu.VMEM((ROWS, SEQ * GROUP, HD), BF16),
            pltpu.VMEM((ROWS, SEQ, 2 * HD), BF16),
            pltpu.VMEM((SEQ, GROUP, ROWS, HD), BF16),
            pltpu.VMEM((SEQ, ROWS, 2 * HD), BF16),
            pltpu.SMEM((32, 32), jnp.int32),
            pltpu.SMEM((32,), jnp.int32),
            pltpu.VMEM((SEQ, GROUP, ROWS, HD), BF16),
            pltpu.VMEM((SEQ, GROUP, ROWS, HD), BF16),
            pltpu.VMEM((2, 4, GROUP, ROWS, HD), BF16),
            pltpu.VMEM((SEQ, GROUP, ROWS, HD), F32),
            pltpu.VMEM((8, QROWS), F32),
            pltpu.VMEM((8, QROWS), F32),
            pltpu.VMEM((2, 8, QROWS), F32),
            pltpu.VMEM((SEQ, ROWS, 2 * HD), BF16),
            pltpu.VMEM((SEQ, GROUP, ROWS, HD), BF16),
            pltpu.VMEM((HD, QROWS), BF16),
            pltpu.VMEM((32, 2 * CT, HD), BF16),
            pltpu.VMEM((HD, QROWS), F32),
            pltpu.VMEM((1, QROWS), F32),
            pltpu.VMEM((1, QROWS), F32),
            pltpu.VMEM((SEQ, GROUP, ROWS, HD), BF16),
            pltpu.VMEM((4, GROUP, ROWS, HD), BF16),
            pltpu.VMEM((2, 4 * ROWS, CT), BF16),
            pltpu.VMEM((BLOCKS, CT, CT), BF16),
            pltpu.VMEM((BLOCKS, CT, CT), BF16),
            pltpu.VMEM((2, NC, 4, ROWS, CT), F32),
            pltpu.VMEM((3, 2, NC, ROWS, CT), BF16),
            pltpu.VMEM((3, 2, NC, ROWS, CT), BF16),
            pltpu.VMEM((ROWS, D), BF16),
            pltpu.VMEM((64, D), F32),
            pltpu.VMEM((ROWS, D), BF16),
            dma((6,)), dma((6,)), dma((SEQ,)), dma((SEQ,)), dma((SEQ,)), dma((SEQ,)),
            dma((4,)), dma((1,)), dma((4, 2)), dma((4, 2)), dma((16,)), dma((32,)), dma((4, 2)),
            dma((BLOCKS + 6,)), dma((2,)), dma((2, 4)), dma((8,)), dma((BLOCKS,)), dma((2,)),
            dma((3, 2, NC)), dma((3, 2, NC)), dma((BLOCKS,)), dma((BLOCKS,)),
        ],
        compiler_params=pltpu.CompilerParams(
            collective_id=0, has_side_effects=True, vmem_limit_bytes=60 * MIB
        ),
        cost_estimate=pl.CostEstimate(
            flops=4 * QROWS * HD * CT * 24, bytes_accessed=20 * MIB, transcendentals=QROWS * CT * 24
        ),
        name="stretch_attention",
    )(queries, keys_values, mask, level, own, latents, gate_table)


def on_device(queries, keys_values, out_weight, latents, gate_table, noise_level, stretch_mask):
    return fused(queries, keys_values, stretch_mask, noise_level, out_weight, latents, gate_table)


def solution(mesh):
    rows = P(("stretch", "seq"), None)
    heads = P(("stretch", "seq"), None, None)
    return jax.shard_map(
        on_device,
        mesh=mesh,
        in_specs=(heads, heads, P("seq", None), rows, P(), P(), P()),
        out_specs=rows,
        check_vma=False,
    )
```
